32 devices in a mesh: groups: 2 (over x), seq: 16 (over z, y, core).
Axes of the slice: x: 2, y: 2, z: 4, core: 2. Of those that a mesh axis runs over, the one named last changes fastest.
Arguments:
- queries: bfloat16 [16384, 2048], P(('groups', 'seq')), parts along dimension 0, may hold values from -8 to 8
- keys: bfloat16 [16384, 512], P(('groups', 'seq')), parts along dimension 0, may hold values from -8 to 8
- values: bfloat16 [16384, 512], P(('groups', 'seq')), parts along dimension 0, may hold values from -6 to 6
- block_table: int32 [128, 8], P(('groups', 'seq')), parts along dimension 0, may hold values from 0 to 63, as said below
- out_weight: bfloat16 [2048, 4096], P('seq'), may hold values from -0.125 to 0.125
Outputs:
- projected: bfloat16 [16384, 4096], P(('groups', 'seq')), parts along dimension 0
The draws below stay inside these ranges and needn't reach their ends.
There are 2 independent parts, one for each index of `groups`. The reference program is written for one: setup_inputs(seed, part) draws one part's arguments, and reference() takes and returns one part's arrays. A program takes and returns all parts, laid end to end along the dimension named above; an argument that names none is the same for every part. Nothing has to cross between parts.
Inputs may be any that keep to these rules, and one draw needn't show every extreme that they name: `block_table`: entry j of the row of query block b names a key block held by index (b // 4 + j * 2 - ((b mod 4) mod 2)) mod 16 of seq, that is a block number s * 4 + r with that index s and 0 <= r < 4.
All inputs are finite; a program needn't handle non-finite values.
Results may differ from the reference program's by a relative error of at most 0.013.
Values may be sent and summed in bfloat16 or wider, within the bound.
A program may use at most 320 MiB of HBM per device.

```python
import jax
import jax.numpy as jnp
from jax import lax

D = 4096
H = 16
KVH = 4
HD = 128
QB = 128
ENTRIES = 8
TOKENS = 8192
NQB = 64
BPS = 4
STRIDE = 2


def draw_queries(key, part):
    shape = (TOKENS, KVH, H // KVH, HD)
    base = jnp.clip(jax.random.normal(jax.random.fold_in(key, 11), shape, jnp.float32), -6.0, 6.0)
    return base.reshape(TOKENS, H * HD).astype(jnp.bfloat16)


def draw_keys(key, part):
    shape = (TOKENS, KVH, HD)
    base = jnp.clip(jax.random.normal(jax.random.fold_in(key, 13), shape, jnp.float32), -6.0, 6.0)
    return base.reshape(TOKENS, KVH * HD).astype(jnp.bfloat16)


def draw_block_table(key, part):
    shards = NQB // BPS
    rows = jnp.arange(NQB, dtype=jnp.int32)
    entry = jnp.arange(ENTRIES, dtype=jnp.int32)
    lag = rows % BPS % 2
    target = (rows[:, None] // BPS + entry[None, :] * STRIDE - lag[:, None] + shards) % shards
    within = jax.random.randint(jax.random.fold_in(key, 17), (NQB, ENTRIES), 0, BPS, jnp.int32)
    within = within.at[0, 0].set(0).at[NQB - BPS, 0].set(BPS - 1)
    return (target * BPS + within).astype(jnp.int32)


def shard_levels(rng, extent, cuts, smallest, high):
    level, own = 1.0, jax.random.fold_in(rng, 6)
    for dim, blocks in cuts:
        steps = jnp.exp(jax.random.uniform(jax.random.fold_in(own, dim), (blocks,), jnp.float32, smallest / len(cuts), high / len(cuts)))
        level = level * jnp.repeat(steps, extent[dim] // blocks).reshape([-1 if axis == dim else 1 for axis in range(len(extent))])
    return level


def normal_values(rng, extent, width, limit, pieces=(), kind=jnp.bfloat16):
    values = jax.random.normal(rng, extent, jnp.float32) * width
    if len(pieces) > 0:
        values = shard_levels(rng, extent, pieces, -0.22, 0.18) * values
    return jnp.clip(values, min=-limit, max=limit).astype(kind)


def setup_inputs(seed: int = 0, part: int = 0) -> dict:
    key_list = jax.random.split(jax.random.key(seed), 6)
    part_splits = jax.random.split(jax.random.fold_in(key_list[5], part), 6)
    return {
        "queries": draw_queries(jax.random.fold_in(jax.random.fold_in(key_list[5], part), 71), part),
        "keys": draw_keys(jax.random.fold_in(jax.random.fold_in(key_list[5], part), 71), part),
        "values": normal_values(part_splits[2], (TOKENS, KVH * HD), 1.0, 6.0, ((0, 16),)),
        "block_table": draw_block_table(jax.random.fold_in(jax.random.fold_in(key_list[5], part), 71), part),
        "out_weight": normal_values(key_list[4], (H * HD, D), (H * HD) ** -0.5, 0.125, ((0, 16),)),
    }


def reference(queries, keys, values, block_table, out_weight):
    groups = H // KVH
    key_blocks = keys.reshape(NQB, QB, KVH, HD)
    value_blocks = values.reshape(NQB, QB, KVH, HD)
    query_blocks = queries.reshape(NQB, QB, KVH, groups, HD)
    scale = HD ** -0.5

    def one_block(packed):
        query, picks = packed
        key_set = key_blocks[picks].reshape(ENTRIES * QB, KVH, HD).astype(jnp.float32)
        value_set = value_blocks[picks].reshape(ENTRIES * QB, KVH, HD).astype(jnp.float32)
        scores = jnp.einsum("qkgd,skd->kgqs", query.astype(jnp.float32), key_set) * scale
        highest = jnp.max(scores, axis=-1, keepdims=True)
        weights = jnp.exp(scores - highest)
        total = jnp.sum(weights, axis=-1)
        rounded = lax.optimization_barrier(weights.astype(jnp.bfloat16)).astype(jnp.float32)
        mixed = jnp.einsum("kgqs,skd->qkgd", rounded, value_set)
        mixed = mixed / jnp.moveaxis(total, 2, 0)[..., None]
        return mixed.reshape(QB, H * HD).astype(jnp.bfloat16)

    attended = lax.map(one_block, (query_blocks, block_table)).reshape(TOKENS, H * HD)
    return jnp.dot(attended, out_weight, preferred_element_type=jnp.float32).astype(jnp.bfloat16)
```

```python
import functools

import jax
import jax.numpy as jnp
from jax import lax
from jax.experimental import pallas as pl
from jax.experimental.pallas import tpu as pltpu
from jax.sharding import PartitionSpec as P

H = 16
KVH = 4
HD = 128
QB = 128
ENTRIES = 8
MESH = pl.DeviceIdType.MESH
LOG2E = 1.4426950408889634


def kernel(
    Z, Y, q_ref, k_ref, v_ref, t_ref, w_ref, o_ref,
    q_all, kv, t_all, t_smem, w_all, att, att_full, send, recv, local,
):
    cell = 2 * Y
    hp = KVH // cell
    gh = H // KVH
    tok = q_ref.shape[0]
    nq = tok // QB
    wrows = w_ref.shape[0]
    half = wrows // 2
    qc = hp * gh * HD
    kc = hp * HD

    g = lax.axis_index("groups")
    s = lax.axis_index("seq")
    z = lax.div(s, cell)
    i = lax.rem(s, cell)
    y = lax.div(i, 2)
    c = lax.rem(i, 2)
    xh = lax.rem(g, 2)
    gx = g + 1 - 2 * xh

    def dev(dy, dc):
        yy = 1 - y if dy else y
        cc = 1 - c if dc else c
        return yy * 2 + cc

    cores = i - c + (1 - c)
    partners = [dev(dy, dc) for dy in range(Y - 1, -1, -1) for dc in (1, 0) if dy or dc]
    has_left = z > 0
    has_right = z < Z - 1

    counter = [0]

    def new_id():
        counter[0] += 1
        return counter[0] - 1

    def rcopy(n, src, dst, gg, ss):
        return pltpu.make_async_remote_copy(
            src_ref=src, dst_ref=dst, send_sem=send.at[n], recv_sem=recv.at[n],
            device_id=(gg, ss), device_id_type=MESH,
        )

    pending = []

    barrier = pltpu.get_barrier_semaphore()
    for p in partners:
        pl.semaphore_signal(barrier, inc=1, device_id=(g, z * cell + p), device_id_type=MESH)
    pl.semaphore_signal(barrier, inc=1, device_id=(gx, s), device_id_type=MESH)

    @pl.when(has_left)
    def _():
        pl.semaphore_signal(barrier, inc=1, device_id=(g, s - cell), device_id_type=MESH)

    @pl.when(has_right)
    def _():
        pl.semaphore_signal(barrier, inc=1, device_id=(g, s + cell), device_id_type=MESH)

    edges = jnp.where(has_left, 1, 0) + jnp.where(has_right, 1, 0)
    pl.semaphore_wait(barrier, len(partners) + 1 + edges)

    def wunit(origin, idx, xx, rows=None):
        start = (origin * cell + idx) * wrows + xx * half
        return w_all.at[pl.ds(pl.multiple_of(start, 16), half), :]

    def wpair(origin, idx):
        start = (origin * cell + idx) * wrows
        return w_all.at[pl.ds(pl.multiple_of(start, 16), wrows), :]

    def layer_rows(origin):
        n = cell * nq
        return kv.at[:, pl.ds(origin * n, n)]

    def z_copies(ids, src_of, dst_of, t):
        right = (has_right & (z - t >= 0), lambda: rcopy(ids[0], src_of(z - t), dst_of(z - t), g, s + cell))
        left = (has_left & (z + t <= Z - 1), lambda: rcopy(ids[1], src_of(z + t), dst_of(z + t), g, s - cell))
        from_left = (z - 1 - t >= 0, lambda: rcopy(ids[0], dst_of(z - 1 - t), dst_of(z - 1 - t), g, s + cell))
        from_right = (z + 1 + t <= Z - 1, lambda: rcopy(ids[1], dst_of(z + 1 + t), dst_of(z + 1 + t), g, s - cell))
        return (right, left), (from_left, from_right)

    def start_if(cond, make):
        @pl.when(cond)
        def _():
            make().start()

        pending.append((cond, make))

    def start(make):
        make().start()
        pending.append((None, make))

    def wait_recv_if(cond, make):
        @pl.when(cond)
        def _():
            make().wait_recv()

    loc = [
        pltpu.make_async_copy(k_ref.at[:, :, pl.ds(pl.multiple_of(i * kc, 128), kc)],
                              kv.at[0, pl.ds(s * nq, nq)], local.at[0]),
        pltpu.make_async_copy(v_ref.at[:, :, pl.ds(pl.multiple_of(i * kc, 128), kc)],
                              kv.at[1, pl.ds(s * nq, nq)], local.at[1]),
        pltpu.make_async_copy(q_ref.at[:, pl.ds(pl.multiple_of(i * qc, 128), qc)],
                              q_all.at[pl.ds(pl.multiple_of(i * tok, 128), tok), :], local.at[2]),
        pltpu.make_async_copy(t_ref, t_all.at[i], local.at[3]),
        pltpu.make_async_copy(w_ref, wpair(z, i), local.at[4]),
    ]
    for cp in loc:
        cp.start()

    def w_src0(origin):
        return w_ref.at[pl.ds(pl.multiple_of(xh * half, 16), half), :]

    wz_ids = [(new_id(), new_id()) for _ in range(Z - 1)]
    kz_ids = [(new_id(), new_id()) for _ in range(Z - 1)]

    def wz(t):
        if t == 0:
            dst = lambda origin: wunit(origin, i, xh)
            return z_copies(wz_ids[0], w_src0, dst, 0)
        same = lambda origin: wunit(origin, i, xh)
        return z_copies(wz_ids[t], same, same, t)

    def kz(t):
        return z_copies(kz_ids[t], layer_rows, layer_rows, t)

    for cond, make in wz(0)[0]:
        start_if(cond, make)

    kv_in, q_in, t_in = [], [], []
    for p in partners:
        for which, ref in ((0, k_ref), (1, v_ref)):
            n = new_id()

            def make(n=n, p=p, which=which, ref=ref):
                return rcopy(n, ref.at[:, :, pl.ds(pl.multiple_of(p * kc, 128), kc)],
                             kv.at[which, pl.ds(s * nq, nq)], g, z * cell + p)

            def landed(n=n, p=p, which=which):
                at = kv.at[which, pl.ds((z * cell + p) * nq, nq)]
                return rcopy(n, at, at, g, z * cell + p)

            start(make)
            kv_in.append(landed)
    def w_send(make_src, make_dst, gg, ss, make_land, cond=None):
        n = new_id()
        make = lambda: rcopy(n, make_src(), make_dst(), gg, ss)
        if cond is None:
            start(make)
        else:
            start_if(cond, make)
        return (cond, lambda: rcopy(n, make_land(), make_land(), gg, ss))

    yi = (1 - y) * 2 + c
    core_dev = z * cell + cores
    y_dev = z * cell + yi
    y_cores = (1 - y) * 2 + (1 - c)

    def send_core(origin, idx, xx, idx_there, xx_there, cond=None):
        return w_send(lambda: wunit(origin, idx, xx), lambda: wunit(origin, idx, xx), g, core_dev,
                      lambda: wunit(origin, idx_there, xx_there), cond)

    final = []
    n_own = new_id()
    own_core = lambda: rcopy(n_own, w_ref, wpair(z, i), g, core_dev)
    start(own_core)
    final.append((None, lambda: rcopy(n_own, wpair(z, cores), wpair(z, cores), g, core_dev)))
    y_lands = []
    if Y == 2:
        y_lands.append((z, None, w_send(lambda: w_src0(z), lambda: wunit(z, i, xh), g, y_dev,
                                        lambda: wunit(z, yi, xh))))
    for p in partners:
        n = new_id()

        def make(n=n, p=p):
            return rcopy(n, q_ref.at[:, pl.ds(pl.multiple_of(p * qc, 128), qc)],
                         q_all.at[pl.ds(pl.multiple_of(i * tok, 128), tok), :], g, z * cell + p)

        def landed(n=n, p=p):
            at = q_all.at[pl.ds(pl.multiple_of(p * tok, 128), tok), :]
            return rcopy(n, at, at, g, z * cell + p)

        start(make)
        q_in.append(landed)
        m = new_id()

        def make_t(m=m, p=p):
            return rcopy(m, t_ref, t_all.at[i], g, z * cell + p)

        def landed_t(m=m, p=p):
            return rcopy(m, t_all.at[p], t_all.at[p], g, z * cell + p)

        start(make_t)
        q_in.append(landed_t)

    x_lands = []

    def spread(origin, cond):
        x_lands.append((origin, cond, i, w_send(
            lambda: wunit(origin, i, xh), lambda: wunit(origin, i, xh), gx, s,
            lambda: wunit(origin, i, 1 - xh), cond)))
        if Y == 2:
            y_lands.append((origin, cond, w_send(
                lambda: wunit(origin, i, xh), lambda: wunit(origin, i, xh), g, y_dev,
                lambda: wunit(origin, yi, xh), cond)))
        final.append(send_core(origin, i, xh, cores, xh, cond))

    def maybe_wait(entry):
        cond, make = entry
        if cond is None:
            make().wait_recv()
        else:
            wait_recv_if(cond, make)

    def relay_y():
        while y_lands:
            origin, cond, entry = y_lands.pop(0)
            maybe_wait(entry)
            x_lands.append((origin, cond, yi, w_send(
                lambda origin=origin: wunit(origin, yi, xh), lambda origin=origin: wunit(origin, yi, xh), gx, s,
                lambda origin=origin: wunit(origin, yi, 1 - xh), cond)))
            final.append(send_core(origin, yi, xh, y_cores, xh, cond))

    def relay_x():
        while x_lands:
            origin, cond, idx, entry = x_lands.pop(0)
            maybe_wait(entry)
            there = cores if idx is i else y_cores
            final.append(send_core(origin, idx, 1 - xh, there, 1 - xh, cond))

    def w_step(t):
        for cond, make in wz(t)[1]:
            wait_recv_if(cond, make)
        if t + 1 < Z - 1:
            for cond, make in wz(t + 1)[0]:
                start_if(cond, make)
        spread(z - 1 - t, z - 1 - t >= 0)
        spread(z + 1 + t, z + 1 + t <= Z - 1)

    def k_step(t):
        for cond, make in kz(t)[1]:
            wait_recv_if(cond, make)
        if t + 1 < Z - 1:
            for cond, make in kz(t + 1)[0]:
                start_if(cond, make)

    w_step(0)
    for make in kv_in:
        make().wait_recv()
    for cp in loc:
        cp.wait()
    for cond, make in kz(0)[0]:
        start_if(cond, make)
    for t in range(1, Z - 1):
        w_step(t)
    k_step(0)
    relay_y()
    for t in range(1, Z - 1):
        k_step(t)
    relay_x()

    for make in q_in:
        make().wait_recv()
    tcp = pltpu.make_async_copy(t_all, t_smem, local.at[5])
    tcp.start()
    tcp.wait()

    factor = HD ** -0.5 * LOG2E

    def attend(owner):
        def block(b, carry):
            rows = pl.ds(pl.multiple_of(owner * tok + b * QB, QB), QB)
            ids = [t_smem[owner, b, e] for e in range(ENTRIES)]
            for hh in range(hp):
                kcols = pl.ds(hh * HD, HD)
                keys = jnp.concatenate([kv[0, n, :, kcols] for n in ids], 0)
                vals = jnp.concatenate([kv[1, n, :, kcols] for n in ids], 0)
                for pair in range(gh // 2):
                    cols = [pl.ds((hh * gh + pair * 2 + h) * HD, HD) for h in range(2)]
                    qq = jnp.concatenate([q_all[rows, cc] for cc in cols], 0)
                    sc = lax.dot_general(qq, keys, (((1,), (1,)), ((), ())),
                                         preferred_element_type=jnp.float32)
                    top = jnp.max(sc, axis=-1, keepdims=True)
                    wts = jnp.exp2((sc - top) * factor)
                    total = jnp.sum(wts, axis=-1, keepdims=True)
                    mixed = jnp.dot(wts.astype(jnp.bfloat16), vals, preferred_element_type=jnp.float32)
                    mixed = (mixed / total).astype(jnp.bfloat16)
                    for h in range(2):
                        att[rows, cols[h]] = mixed[h * QB:(h + 1) * QB]
            return carry

        lax.fori_loop(0, nq, block, 0)

    att_in = []
    for p in partners:
        attend(p)
        n = new_id()

        def make(n=n, p=p):
            return rcopy(n, att.at[pl.ds(pl.multiple_of(p * tok, 128), tok), :],
                         att_full.at[:, pl.ds(pl.multiple_of(i * qc, 128), qc)], g, z * cell + p)

        def landed(n=n, p=p):
            at = att_full.at[:, pl.ds(pl.multiple_of(p * qc, 128), qc)]
            return rcopy(n, at, at, g, z * cell + p)

        start(make)
        att_in.append(landed)
    attend(i)
    own = pltpu.make_async_copy(att.at[pl.ds(pl.multiple_of(i * tok, 128), tok), :],
                                att_full.at[:, pl.ds(pl.multiple_of(i * qc, 128), qc)], local.at[6])
    own.start()
    own.wait()
    for make in att_in:
        make().wait_recv()
    for entry in final:
        maybe_wait(entry)

    tile = 512
    def project(j, carry):
        cols = pl.ds(pl.multiple_of(j * tile, tile), tile)
        o_ref[:, cols] = jnp.dot(att_full[...], w_all[:, cols],
                                 preferred_element_type=jnp.float32).astype(jnp.bfloat16)
        return carry

    lax.fori_loop(0, o_ref.shape[1] // tile, project, 0)
    for cond, make in pending:
        if cond is None:
            make().wait_send()
        else:
            @pl.when(cond)
            def _(make=make):
                make().wait_send()


def body(Z, Y, queries, keys, values, block_table, out_weight):
    tok, width = queries.shape
    cell = 2 * Y
    hp = KVH // cell
    D = out_weight.shape[1]
    table = jnp.pad(block_table, ((0, 8 - block_table.shape[0]), (0, 128 - ENTRIES)))
    blocks = (tok // QB, QB, KVH * HD)
    steps = Z - 1
    n_sems = steps * 4 + (cell - 1) * 5 + 8 + steps * 2 * 9
    flops = 2 * tok * width * D + 4 * tok * H * ENTRIES * QB * HD
    return pl.pallas_call(
        functools.partial(kernel, Z, Y),
        out_shape=jax.ShapeDtypeStruct((tok, D), jnp.bfloat16),
        in_specs=[pl.BlockSpec(memory_space=pl.ANY)] * 5,
        out_specs=pl.BlockSpec(memory_space=pltpu.VMEM),
        scratch_shapes=[
            pltpu.VMEM((cell * tok, width // cell), jnp.bfloat16),
            pltpu.VMEM((2, Z * cell * tok // QB, QB, hp * HD), jnp.bfloat16),
            pltpu.VMEM((cell, 8, 128), jnp.int32),
            pltpu.SMEM((cell, 8, 128), jnp.int32),
            pltpu.VMEM((out_weight.shape[0] * Z * cell, D), jnp.bfloat16),
            pltpu.VMEM((cell * tok, width // cell), jnp.bfloat16),
            pltpu.VMEM((tok, width), jnp.bfloat16),
            pltpu.SemaphoreType.DMA((n_sems,)),
            pltpu.SemaphoreType.DMA((n_sems,)),
            pltpu.SemaphoreType.DMA((7,)),
        ],
        compiler_params=pltpu.CompilerParams(
            collective_id=0, has_side_effects=True, vmem_limit_bytes=58 * 1024 * 1024,
        ),
        cost_estimate=pl.CostEstimate(flops=flops, bytes_accessed=64 * 1024 * 1024, transcendentals=0),
    )(queries, keys.reshape(blocks), values.reshape(blocks), table, out_weight)


def solution(mesh):
    groups, seq = mesh.shape["groups"], mesh.shape["seq"]
    Y = 2 if groups == 2 else 1
    Z = seq // (2 * Y)
    in_specs = (
        P(("groups", "seq"), None),
        P(("groups", "seq"), None),
        P(("groups", "seq"), None),
        P(("groups", "seq"), None),
        P("seq", None),
    )
    return jax.shard_map(
        functools.partial(body, Z, Y), mesh=mesh, in_specs=in_specs,
        out_specs=P(("groups", "seq"), None), check_vma=False,
    )
```

```python
import functools

import jax
import jax.numpy as jnp
from jax import lax
from jax.experimental import pallas as pl
from jax.experimental.pallas import tpu as pltpu
from jax.sharding import PartitionSpec as P

H = 16
KVH = 4
HD = 128
QB = 128
ENTRIES = 8
MESH = pl.DeviceIdType.MESH
LOG2E = 1.4426950408889634


def kernel(
    Z, Y, online, q_ref, k_ref, v_ref, t_ref, w_ref, o_ref,
    q_all, kv, kv_left, kv_right, t_all, t_smem, w_all, att, att_full, m_ref, l_ref, acc_ref, send, recv, local,
):
    cell = 2 * Y
    hp = KVH // cell
    gh = H // KVH
    tok = q_ref.shape[0]
    nq = tok // QB
    wrows = w_ref.shape[0]
    half = wrows // 2
    qc = hp * gh * HD
    kc = hp * HD

    g = lax.axis_index("groups")
    s = lax.axis_index("seq")
    z = lax.div(s, cell)
    i = lax.rem(s, cell)
    y = lax.div(i, 2)
    c = lax.rem(i, 2)
    xh = lax.rem(g, 2)
    gx = g + 1 - 2 * xh

    def dev(dy, dc):
        yy = 1 - y if dy else y
        cc = 1 - c if dc else c
        return yy * 2 + cc

    cores = i - c + (1 - c)
    partners = [dev(dy, dc) for dy in range(Y - 1, -1, -1) for dc in (1, 0) if dy or dc]
    has_left = z > 0
    has_right = z < Z - 1

    counter = [0]

    def new_id():
        counter[0] += 1
        return counter[0] - 1

    def rcopy(n, src, dst, gg, ss):
        return pltpu.make_async_remote_copy(
            src_ref=src, dst_ref=dst, send_sem=send.at[n], recv_sem=recv.at[n],
            device_id=(gg, ss), device_id_type=MESH,
        )

    pending = []

    barrier = pltpu.get_barrier_semaphore()
    for p in partners:
        pl.semaphore_signal(barrier, inc=1, device_id=(g, z * cell + p), device_id_type=MESH)
    pl.semaphore_signal(barrier, inc=1, device_id=(gx, s), device_id_type=MESH)

    @pl.when(has_left)
    def _():
        pl.semaphore_signal(barrier, inc=1, device_id=(g, s - cell), device_id_type=MESH)

    @pl.when(has_right)
    def _():
        pl.semaphore_signal(barrier, inc=1, device_id=(g, s + cell), device_id_type=MESH)

    edges = jnp.where(has_left, 1, 0) + jnp.where(has_right, 1, 0)
    pl.semaphore_wait(barrier, len(partners) + 1 + edges)

    def wunit(origin, idx, xx, rows=None):
        start = (origin * cell + idx) * wrows + xx * half
        return w_all.at[pl.ds(pl.multiple_of(start, 16), half), :]

    def wpair(origin, idx):
        start = (origin * cell + idx) * wrows
        return w_all.at[pl.ds(pl.multiple_of(start, 16), wrows), :]

    def layer_rows(origin):
        n = cell * nq
        return kv.at[:, pl.ds(origin * n, n)]

    def own_blocks(which, idx):
        return kv.at[which, pl.ds((idx if online else z * cell + idx) * nq, nq)]

    def z_copies(ids, src_of, dst_of, t):
        right = (has_right & (z - t >= 0), lambda: rcopy(ids[0], src_of(z - t), dst_of(z - t), g, s + cell))
        left = (has_left & (z + t <= Z - 1), lambda: rcopy(ids[1], src_of(z + t), dst_of(z + t), g, s - cell))
        from_left = (z - 1 - t >= 0, lambda: rcopy(ids[0], dst_of(z - 1 - t), dst_of(z - 1 - t), g, s + cell))
        from_right = (z + 1 + t <= Z - 1, lambda: rcopy(ids[1], dst_of(z + 1 + t), dst_of(z + 1 + t), g, s - cell))
        return (right, left), (from_left, from_right)

    def start_if(cond, make):
        @pl.when(cond)
        def _():
            make().start()

        pending.append((cond, make))

    def start(make):
        make().start()
        pending.append((None, make))

    def wait_recv_if(cond, make):
        @pl.when(cond)
        def _():
            make().wait_recv()

    loc = [
        pltpu.make_async_copy(k_ref.at[:, :, pl.ds(pl.multiple_of(i * kc, 128), kc)],
                              own_blocks(0, i), local.at[0]),
        pltpu.make_async_copy(v_ref.at[:, :, pl.ds(pl.multiple_of(i * kc, 128), kc)],
                              own_blocks(1, i), local.at[1]),
        pltpu.make_async_copy(q_ref.at[:, pl.ds(pl.multiple_of(i * qc, 128), qc)],
                              q_all.at[pl.ds(pl.multiple_of(i * tok, 128), tok), :], local.at[2]),
        pltpu.make_async_copy(t_ref, t_all.at[i], local.at[3]),
        pltpu.make_async_copy(w_ref, wpair(z, i), local.at[4]),
    ]
    for cp in loc:
        cp.start()

    def w_src0(origin):
        return w_ref.at[pl.ds(pl.multiple_of(xh * half, 16), half), :]

    wz_ids = [(new_id(), new_id()) for _ in range(Z - 1)]
    kz_ids = [(new_id(), new_id()) for _ in range(Z - 1)]

    def wz(t):
        if t == 0:
            dst = lambda origin: wunit(origin, i, xh)
            return z_copies(wz_ids[0], w_src0, dst, 0)
        same = lambda origin: wunit(origin, i, xh)
        return z_copies(wz_ids[t], same, same, t)

    def kz(t):
        if online:
            ids = kz_ids[t]
            to_right = lambda: rcopy(ids[0], kv_left[t - 1] if t else kv, kv_left[t], g, s + cell)
            to_left = lambda: rcopy(ids[1], kv_right[t - 1] if t else kv, kv_right[t], g, s - cell)
            right = (has_right & (z - t >= 0), to_right)
            left = (has_left & (z + t <= Z - 1), to_left)
            return (right, left), ((z - 1 - t >= 0, to_right), (z + 1 + t <= Z - 1, to_left))
        return z_copies(kz_ids[t], layer_rows, layer_rows, t)

    for cond, make in wz(0)[0]:
        start_if(cond, make)

    kv_in, q_in, t_in = [], [], []
    for p in partners:
        for which, ref in ((0, k_ref), (1, v_ref)):
            n = new_id()

            def make(n=n, p=p, which=which, ref=ref):
                return rcopy(n, ref.at[:, :, pl.ds(pl.multiple_of(p * kc, 128), kc)],
                             own_blocks(which, i), g, z * cell + p)

            def landed(n=n, p=p, which=which):
                at = own_blocks(which, p)
                return rcopy(n, at, at, g, z * cell + p)

            start(make)
            kv_in.append(landed)
    def w_send(make_src, make_dst, gg, ss, make_land, cond=None):
        n = new_id()
        make = lambda: rcopy(n, make_src(), make_dst(), gg, ss)
        if cond is None:
            start(make)
        else:
            start_if(cond, make)
        return (cond, lambda: rcopy(n, make_land(), make_land(), gg, ss))

    yi = (1 - y) * 2 + c
    core_dev = z * cell + cores
    y_dev = z * cell + yi
    y_cores = (1 - y) * 2 + (1 - c)

    def send_core(origin, idx, xx, idx_there, xx_there, cond=None):
        return w_send(lambda: wunit(origin, idx, xx), lambda: wunit(origin, idx, xx), g, core_dev,
                      lambda: wunit(origin, idx_there, xx_there), cond)

    final = []
    n_own = new_id()
    own_core = lambda: rcopy(n_own, w_ref, wpair(z, i), g, core_dev)
    start(own_core)
    final.append((None, lambda: rcopy(n_own, wpair(z, cores), wpair(z, cores), g, core_dev)))
    y_lands = []
    if Y == 2:
        y_lands.append((z, None, w_send(lambda: w_src0(z), lambda: wunit(z, i, xh), g, y_dev,
                                        lambda: wunit(z, yi, xh))))
    for p in partners:
        n = new_id()

        def make(n=n, p=p):
            return rcopy(n, q_ref.at[:, pl.ds(pl.multiple_of(p * qc, 128), qc)],
                         q_all.at[pl.ds(pl.multiple_of(i * tok, 128), tok), :], g, z * cell + p)

        def landed(n=n, p=p):
            at = q_all.at[pl.ds(pl.multiple_of(p * tok, 128), tok), :]
            return rcopy(n, at, at, g, z * cell + p)

        start(make)
        q_in.append(landed)
        m = new_id()

        def make_t(m=m, p=p):
            return rcopy(m, t_ref, t_all.at[i], g, z * cell + p)

        def landed_t(m=m, p=p):
            return rcopy(m, t_all.at[p], t_all.at[p], g, z * cell + p)

        start(make_t)
        q_in.append(landed_t)

    x_lands = []

    def spread(origin, cond):
        x_lands.append((origin, cond, i, w_send(
            lambda: wunit(origin, i, xh), lambda: wunit(origin, i, xh), gx, s,
            lambda: wunit(origin, i, 1 - xh), cond)))
        if Y == 2:
            y_lands.append((origin, cond, w_send(
                lambda: wunit(origin, i, xh), lambda: wunit(origin, i, xh), g, y_dev,
                lambda: wunit(origin, yi, xh), cond)))
        final.append(send_core(origin, i, xh, cores, xh, cond))

    def maybe_wait(entry):
        cond, make = entry
        if cond is None:
            make().wait_recv()
        else:
            wait_recv_if(cond, make)

    def relay_y(count=1 << 20):
        while y_lands and count > 0:
            count -= 1
            origin, cond, entry = y_lands.pop(0)
            maybe_wait(entry)
            x_lands.append((origin, cond, yi, w_send(
                lambda origin=origin: wunit(origin, yi, xh), lambda origin=origin: wunit(origin, yi, xh), gx, s,
                lambda origin=origin: wunit(origin, yi, 1 - xh), cond)))
            final.append(send_core(origin, yi, xh, y_cores, xh, cond))

    def relay_x(count=1 << 20):
        while x_lands and count > 0:
            count -= 1
            origin, cond, idx, entry = x_lands.pop(0)
            maybe_wait(entry)
            there = cores if idx is i else y_cores
            final.append(send_core(origin, idx, 1 - xh, there, 1 - xh, cond))

    def w_step(t):
        for cond, make in wz(t)[1]:
            wait_recv_if(cond, make)
        if t + 1 < Z - 1:
            for cond, make in wz(t + 1)[0]:
                start_if(cond, make)
        spread(z - 1 - t, z - 1 - t >= 0)
        spread(z + 1 + t, z + 1 + t <= Z - 1)

    def k_step(t):
        for cond, make in kz(t)[1]:
            wait_recv_if(cond, make)
        if t + 1 < Z - 1:
            for cond, make in kz(t + 1)[0]:
                start_if(cond, make)

    factor = HD ** -0.5 * LOG2E
    n_seq = Z * cell
    stride = n_seq // ENTRIES

    def softmax_pass(keys, vals, rows, hh, pair, block, first, last):
        cols = [pl.ds((hh * gh + pair * 2 + h) * HD, HD) for h in range(2)]
        qq = jnp.concatenate([q_all[rows, cc] for cc in cols], 0)
        sc = lax.dot_general(qq, keys, (((1,), (1,)), ((), ())), preferred_element_type=jnp.float32)
        top = jnp.max(sc, axis=-1, keepdims=True)
        kept = pl.ds(pl.multiple_of((block * gh + pair * 2) * QB, 2 * QB), 2 * QB)
        if not first:
            before = m_ref[kept, :1]
            top = jnp.maximum(before, top)
        wts = jnp.exp2((sc - top) * factor)
        total = jnp.sum(wts, axis=-1, keepdims=True)
        mixed = jnp.dot(wts.astype(jnp.bfloat16), vals, preferred_element_type=jnp.float32)
        if not first:
            shrink = jnp.exp2((before - top) * factor)
            total = total + l_ref[kept, :1] * shrink
            mixed = mixed + acc_ref[kept, :] * shrink
        if last:
            mixed = (mixed / total).astype(jnp.bfloat16)
            for h in range(2):
                att[rows, cols[h]] = mixed[h * QB:(h + 1) * QB]
        else:
            m_ref[kept, :] = jnp.broadcast_to(top, (2 * QB, HD))
            l_ref[kept, :] = jnp.broadcast_to(total, (2 * QB, HD))
            acc_ref[kept, :] = mixed

    def attend(owner, parts, first, last):
        def step(b, carry):
            rows = pl.ds(pl.multiple_of(owner * tok + b * QB, QB), QB)
            if parts is None:
                picks = [(kv, t_smem[owner, b, e]) for e in range(ENTRIES)]
            else:
                base = z * cell + owner - lax.rem(b, 2) + n_seq
                picks = []
                for ref, layer in parts:
                    for r in range(cell // stride):
                        index = layer * cell + lax.rem(base, stride) + r * stride
                        e = lax.div(lax.rem(index - base + 2 * n_seq, n_seq), stride)
                        picks.append((ref, lax.rem(t_smem[owner, b, e], cell * nq)))
            for hh in range(hp):
                kcols = pl.ds(hh * HD, HD)
                keys = jnp.concatenate([ref[0, n, :, kcols] for ref, n in picks], 0)
                vals = jnp.concatenate([ref[1, n, :, kcols] for ref, n in picks], 0)
                for pair in range(gh // 2):
                    softmax_pass(keys, vals, rows, hh, pair, owner * nq + b, first, last)
            return carry

        lax.fori_loop(0, nq, step, 0)

    def attend_all(parts, first):
        def step(owner, carry):
            attend(owner, parts, first, False)
            return carry

        lax.fori_loop(0, cell, step, 0)

    def if_layer(layer):
        return pl.when(z == layer)

    def attend_last(owner):
        if not online:
            attend(owner, None, True, True)
            return
        for layer in range(Z):
            t = max(layer, Z - 1 - layer) - 1
            part = (kv_left[t], layer - 1 - t) if layer >= Z // 2 else (kv_right[t], layer + 1 + t)

            @if_layer(layer)
            def _(part=part):
                attend(owner, [part], False, True)

    def have_queries():
        for make in q_in:
            make().wait_recv()
        tcp = pltpu.make_async_copy(t_all, t_smem, local.at[5])
        tcp.start()
        tcp.wait()

    w_step(0)
    for make in kv_in:
        make().wait_recv()
    for cp in loc:
        cp.wait()
    for cond, make in kz(0)[0]:
        start_if(cond, make)
    if online:
        w_step(1)
        relay_y(1)
        w_step(2)
        k_step(0)
        relay_y(2)
        have_queries()
        for layer in range(Z):
            parts = [(kv, layer)]
            if layer > 0:
                parts.append((kv_left[0], layer - 1))
            if layer < Z - 1:
                parts.append((kv_right[0], layer + 1))

            @if_layer(layer)
            def _(parts=parts):
                attend_all(parts, True)

        relay_y()
        k_step(1)
        relay_x(4)
        for layer, part in ((0, (kv_right[1], 2)), (Z - 1, (kv_left[1], Z - 3))):

            @if_layer(layer)
            def _(part=part):
                attend_all([part], False)

        relay_x(5)
        k_step(2)
    else:
        for t in range(1, Z - 1):
            w_step(t)
        k_step(0)
        relay_y()
        for t in range(1, Z - 1):
            k_step(t)
        relay_x()
        have_queries()

    att_in = []
    for p in partners:
        attend_last(p)
        n = new_id()

        def make(n=n, p=p):
            return rcopy(n, att.at[pl.ds(pl.multiple_of(p * tok, 128), tok), :],
                         att_full.at[:, pl.ds(pl.multiple_of(i * qc, 128), qc)], g, z * cell + p)

        def landed(n=n, p=p):
            at = att_full.at[:, pl.ds(pl.multiple_of(p * qc, 128), qc)]
            return rcopy(n, at, at, g, z * cell + p)

        start(make)
        att_in.append(landed)
    relay_x()
    attend_last(i)
    own = pltpu.make_async_copy(att.at[pl.ds(pl.multiple_of(i * tok, 128), tok), :],
                                att_full.at[:, pl.ds(pl.multiple_of(i * qc, 128), qc)], local.at[6])
    own.start()
    own.wait()
    for make in att_in:
        make().wait_recv()
    for entry in final:
        maybe_wait(entry)

    tile = 512
    def project(j, carry):
        cols = pl.ds(pl.multiple_of(j * tile, tile), tile)
        o_ref[:, cols] = jnp.dot(att_full[...], w_all[:, cols],
                                 preferred_element_type=jnp.float32).astype(jnp.bfloat16)
        return carry

    lax.fori_loop(0, o_ref.shape[1] // tile, project, 0)
    for cond, make in pending:
        if cond is None:
            make().wait_send()
        else:
            @pl.when(cond)
            def _(make=make):
                make().wait_send()


def body(Z, Y, queries, keys, values, block_table, out_weight):
    tok, width = queries.shape
    cell = 2 * Y
    hp = KVH // cell
    D = out_weight.shape[1]
    table = block_table
    online = Z == 4 and cell % (Z * cell // ENTRIES) == 0
    state = (cell * tok * H // KVH, HD) if online else (8, HD)
    blocks = (tok // QB, QB, KVH * HD)
    part = (2, cell * tok // QB, QB, hp * HD)
    steps = Z - 1
    n_sems = steps * 4 + (cell - 1) * 5 + 8 + steps * 2 * 9
    flops = 2 * tok * width * D + 4 * tok * H * ENTRIES * QB * HD
    return pl.pallas_call(
        functools.partial(kernel, Z, Y, online),
        out_shape=jax.ShapeDtypeStruct((tok, D), jnp.bfloat16),
        in_specs=[pl.BlockSpec(memory_space=pl.ANY)] * 5,
        out_specs=pl.BlockSpec(memory_space=pltpu.VMEM),
        scratch_shapes=[
            pltpu.VMEM((cell * tok, width // cell), jnp.bfloat16),
            pltpu.VMEM(part if online else (2, Z * cell * tok // QB, QB, hp * HD), jnp.bfloat16),
            [pltpu.VMEM(part, jnp.bfloat16)] * (steps if online else 0),
            [pltpu.VMEM(part, jnp.bfloat16)] * (steps if online else 0),
            pltpu.VMEM((cell,) + table.shape, jnp.int32),
            pltpu.SMEM((cell,) + table.shape, jnp.int32),
            pltpu.VMEM((out_weight.shape[0] * Z * cell, D), jnp.bfloat16),
            pltpu.VMEM((cell * tok, width // cell), jnp.bfloat16),
            pltpu.VMEM((tok, width), jnp.bfloat16),
            pltpu.VMEM(state, jnp.float32),
            pltpu.VMEM(state, jnp.float32),
            pltpu.VMEM(state, jnp.float32),
            pltpu.SemaphoreType.DMA((n_sems,)),
            pltpu.SemaphoreType.DMA((n_sems,)),
            pltpu.SemaphoreType.DMA((7,)),
        ],
        compiler_params=pltpu.CompilerParams(
            collective_id=0, has_side_effects=True, vmem_limit_bytes=58 * 1024 * 1024,
        ),
        cost_estimate=pl.CostEstimate(flops=flops, bytes_accessed=64 * 1024 * 1024, transcendentals=0),
    )(queries, keys.reshape(blocks), values.reshape(blocks), table, out_weight)


def solution(mesh):
    groups, seq = mesh.shape["groups"], mesh.shape["seq"]
    Y = 2 if groups == 2 else 1
    Z = seq // (2 * Y)
    in_specs = (
        P(("groups", "seq"), None),
        P(("groups", "seq"), None),
        P(("groups", "seq"), None),
        P(("groups", "seq"), None),
        P("seq", None),
    )
    return jax.shard_map(
        functools.partial(body, Z, Y), mesh=mesh, in_specs=in_specs,
        out_specs=P(("groups", "seq"), None), check_vma=False,
    )
```

```python
import functools

import jax
import jax.numpy as jnp
from jax import lax
from jax.experimental import pallas as pl
from jax.experimental.pallas import tpu as pltpu
from jax.sharding import PartitionSpec as P

H = 16
KVH = 4
HD = 128
QB = 128
ENTRIES = 8
MESH = pl.DeviceIdType.MESH
LOG2E = 1.4426950408889634


def kernel(
    Z, Y, online, q_ref, k_ref, v_ref, t_ref, w_ref, att_full, w_all,
    q_all, kv, kv_left, kv_right, t_all, t_smem, att, m_ref, l_ref, acc_ref, send, recv, local,
):
    cell = 2 * Y
    hp = KVH // cell
    gh = H // KVH
    tok = q_ref.shape[0]
    nq = tok // QB
    wrows = w_ref.shape[0]
    half = wrows // 2
    qc = hp * gh * HD
    kc = hp * HD

    g = lax.axis_index("groups")
    s = lax.axis_index("seq")
    z = lax.div(s, cell)
    i = lax.rem(s, cell)
    y = lax.div(i, 2)
    c = lax.rem(i, 2)
    xh = lax.rem(g, 2)
    gx = g + 1 - 2 * xh

    def dev(dy, dc):
        yy = 1 - y if dy else y
        cc = 1 - c if dc else c
        return yy * 2 + cc

    cores = i - c + (1 - c)
    partners = [dev(dy, dc) for dy in range(Y - 1, -1, -1) for dc in (1, 0) if dy or dc]
    has_left = z > 0
    has_right = z < Z - 1

    counter = [0]

    def new_id():
        counter[0] += 1
        return counter[0] - 1

    def rcopy(n, src, dst, gg, ss):
        return pltpu.make_async_remote_copy(
            src_ref=src, dst_ref=dst, send_sem=send.at[n], recv_sem=recv.at[n],
            device_id=(gg, ss), device_id_type=MESH,
        )

    pending = []

    barrier = pltpu.get_barrier_semaphore()
    for p in partners:
        pl.semaphore_signal(barrier, inc=1, device_id=(g, z * cell + p), device_id_type=MESH)
    pl.semaphore_signal(barrier, inc=1, device_id=(gx, s), device_id_type=MESH)

    @pl.when(has_left)
    def _():
        pl.semaphore_signal(barrier, inc=1, device_id=(g, s - cell), device_id_type=MESH)

    @pl.when(has_right)
    def _():
        pl.semaphore_signal(barrier, inc=1, device_id=(g, s + cell), device_id_type=MESH)

    edges = jnp.where(has_left, 1, 0) + jnp.where(has_right, 1, 0)
    pl.semaphore_wait(barrier, len(partners) + 1 + edges)

    def wunit(origin, idx, xx, rows=None):
        start = (origin * cell + idx) * wrows + xx * half
        return w_all.at[pl.ds(pl.multiple_of(start, 16), half), :]

    def wpair(origin, idx):
        start = (origin * cell + idx) * wrows
        return w_all.at[pl.ds(pl.multiple_of(start, 16), wrows), :]

    def layer_rows(origin):
        n = cell * nq
        return kv.at[:, pl.ds(origin * n, n)]

    def own_blocks(which, idx):
        return kv.at[which, pl.ds((idx if online else z * cell + idx) * nq, nq)]

    def z_copies(ids, src_of, dst_of, t):
        right = (has_right & (z - t >= 0), lambda: rcopy(ids[0], src_of(z - t), dst_of(z - t), g, s + cell))
        left = (has_left & (z + t <= Z - 1), lambda: rcopy(ids[1], src_of(z + t), dst_of(z + t), g, s - cell))
        from_left = (z - 1 - t >= 0, lambda: rcopy(ids[0], dst_of(z - 1 - t), dst_of(z - 1 - t), g, s + cell))
        from_right = (z + 1 + t <= Z - 1, lambda: rcopy(ids[1], dst_of(z + 1 + t), dst_of(z + 1 + t), g, s - cell))
        return (right, left), (from_left, from_right)

    def start_if(cond, make):
        @pl.when(cond)
        def _():
            make().start()

        pending.append((cond, make))

    def start(make):
        make().start()
        pending.append((None, make))

    def wait_recv_if(cond, make):
        @pl.when(cond)
        def _():
            make().wait_recv()

    loc = [
        pltpu.make_async_copy(k_ref.at[:, :, pl.ds(pl.multiple_of(i * kc, 128), kc)],
                              own_blocks(0, i), local.at[0]),
        pltpu.make_async_copy(v_ref.at[:, :, pl.ds(pl.multiple_of(i * kc, 128), kc)],
                              own_blocks(1, i), local.at[1]),
        pltpu.make_async_copy(q_ref.at[:, pl.ds(pl.multiple_of(i * qc, 128), qc)],
                              q_all.at[pl.ds(pl.multiple_of(i * tok, 128), tok), :], local.at[2]),
        pltpu.make_async_copy(t_ref, t_all.at[i], local.at[3]),
        pltpu.make_async_copy(w_ref, wpair(z, i), local.at[4]),
    ]
    for cp in loc:
        cp.start()

    def w_src0(origin):
        return w_ref.at[pl.ds(pl.multiple_of(xh * half, 16), half), :]

    wz_ids = [(new_id(), new_id()) for _ in range(Z - 1)]
    kz_ids = [(new_id(), new_id()) for _ in range(Z - 1)]

    def wz(t):
        if t == 0:
            dst = lambda origin: wunit(origin, i, xh)
            return z_copies(wz_ids[0], w_src0, dst, 0)
        same = lambda origin: wunit(origin, i, xh)
        return z_copies(wz_ids[t], same, same, t)

    def kz(t):
        if online:
            ids = kz_ids[t]
            to_right = lambda: rcopy(ids[0], kv_left[t - 1] if t else kv, kv_left[t], g, s + cell)
            to_left = lambda: rcopy(ids[1], kv_right[t - 1] if t else kv, kv_right[t], g, s - cell)
            right = (has_right & (z - t >= 0), to_right)
            left = (has_left & (z + t <= Z - 1), to_left)
            return (right, left), ((z - 1 - t >= 0, to_right), (z + 1 + t <= Z - 1, to_left))
        return z_copies(kz_ids[t], layer_rows, layer_rows, t)

    for cond, make in wz(0)[0]:
        start_if(cond, make)

    kv_in = []
    for p in partners:
        for which, ref in ((0, k_ref), (1, v_ref)):
            n = new_id()

            def make(n=n, p=p, which=which, ref=ref):
                return rcopy(n, ref.at[:, :, pl.ds(pl.multiple_of(p * kc, 128), kc)],
                             own_blocks(which, i), g, z * cell + p)

            def landed(n=n, p=p, which=which):
                at = own_blocks(which, p)
                return rcopy(n, at, at, g, z * cell + p)

            start(make)
            kv_in.append(landed)
    def w_send(make_src, make_dst, gg, ss, make_land, cond=None):
        n = new_id()
        make = lambda: rcopy(n, make_src(), make_dst(), gg, ss)
        if cond is None:
            start(make)
        else:
            start_if(cond, make)
        return (cond, lambda: rcopy(n, make_land(), make_land(), gg, ss))

    yi = (1 - y) * 2 + c
    core_dev = z * cell + cores
    y_dev = z * cell + yi
    y_cores = (1 - y) * 2 + (1 - c)

    def send_core(origin, idx, xx, idx_there, xx_there, cond=None):
        return w_send(lambda: wunit(origin, idx, xx), lambda: wunit(origin, idx, xx), g, core_dev,
                      lambda: wunit(origin, idx_there, xx_there), cond)

    final, y_lands, q_in = [], [], []

    def send_rest():
        n_own = new_id()
        own_core = lambda: rcopy(n_own, w_ref, wpair(z, i), g, core_dev)
        start(own_core)
        final.append((None, lambda: rcopy(n_own, wpair(z, cores), wpair(z, cores), g, core_dev)))
        if Y == 2:
            y_lands.append((z, None, w_send(lambda: w_src0(z), lambda: wunit(z, i, xh), g, y_dev,
                                            lambda: wunit(z, yi, xh))))
        for p in partners:
            n = new_id()

            def make(n=n, p=p):
                return rcopy(n, q_ref.at[:, pl.ds(pl.multiple_of(p * qc, 128), qc)],
                             q_all.at[pl.ds(pl.multiple_of(i * tok, 128), tok), :], g, z * cell + p)

            def landed(n=n, p=p):
                at = q_all.at[pl.ds(pl.multiple_of(p * tok, 128), tok), :]
                return rcopy(n, at, at, g, z * cell + p)

            start(make)
            q_in.append(landed)
            m = new_id()

            def make_t(m=m, p=p):
                return rcopy(m, t_ref, t_all.at[i], g, z * cell + p)

            def landed_t(m=m, p=p):
                return rcopy(m, t_all.at[p], t_all.at[p], g, z * cell + p)

            start(make_t)
            q_in.append(landed_t)


    x_lands = []

    def spread(origin, cond):
        x_lands.append((origin, cond, i, w_send(
            lambda: wunit(origin, i, xh), lambda: wunit(origin, i, xh), gx, s,
            lambda: wunit(origin, i, 1 - xh), cond)))
        if Y == 2:
            y_lands.append((origin, cond, w_send(
                lambda: wunit(origin, i, xh), lambda: wunit(origin, i, xh), g, y_dev,
                lambda: wunit(origin, yi, xh), cond)))
        final.append(send_core(origin, i, xh, cores, xh, cond))

    def maybe_wait(entry):
        cond, make = entry
        if cond is None:
            make().wait_recv()
        else:
            wait_recv_if(cond, make)

    def relay_y(count=1 << 20):
        while y_lands and count > 0:
            count -= 1
            origin, cond, entry = y_lands.pop(0)
            maybe_wait(entry)
            x_lands.append((origin, cond, yi, w_send(
                lambda origin=origin: wunit(origin, yi, xh), lambda origin=origin: wunit(origin, yi, xh), gx, s,
                lambda origin=origin: wunit(origin, yi, 1 - xh), cond)))
            final.append(send_core(origin, yi, xh, y_cores, xh, cond))

    def relay_x(count=1 << 20):
        while x_lands and count > 0:
            count -= 1
            origin, cond, idx, entry = x_lands.pop(0)
            maybe_wait(entry)
            there = cores if idx is i else y_cores
            final.append(send_core(origin, idx, 1 - xh, there, 1 - xh, cond))

    def w_step(t):
        for cond, make in wz(t)[1]:
            wait_recv_if(cond, make)
        if t + 1 < Z - 1:
            for cond, make in wz(t + 1)[0]:
                start_if(cond, make)
        spread(z - 1 - t, z - 1 - t >= 0)
        spread(z + 1 + t, z + 1 + t <= Z - 1)

    def k_step(t):
        for cond, make in kz(t)[1]:
            wait_recv_if(cond, make)
        if t + 1 < Z - 1:
            for cond, make in kz(t + 1)[0]:
                start_if(cond, make)

    factor = HD ** -0.5 * LOG2E
    n_seq = Z * cell
    stride = n_seq // ENTRIES

    def softmax_pass(keys, vals, rows, hh, pair, block, first, last):
        cols = [pl.ds((hh * gh + pair * 2 + h) * HD, HD) for h in range(2)]
        qq = jnp.concatenate([q_all[rows, cc] for cc in cols], 0)
        sc = lax.dot_general(qq, keys, (((1,), (1,)), ((), ())), preferred_element_type=jnp.float32)
        top = jnp.max(sc, axis=-1, keepdims=True)
        kept = pl.ds(pl.multiple_of((block * gh + pair * 2) * QB, 2 * QB), 2 * QB)
        if not first:
            before = m_ref[kept, :1]
            top = jnp.maximum(before, top)
        wts = jnp.exp2((sc - top) * factor)
        total = jnp.sum(wts, axis=-1, keepdims=True)
        mixed = jnp.dot(wts.astype(jnp.bfloat16), vals, preferred_element_type=jnp.float32)
        if not first:
            shrink = jnp.exp2((before - top) * factor)
            total = total + l_ref[kept, :1] * shrink
            mixed = mixed + acc_ref[kept, :] * shrink
        if last:
            mixed = (mixed / total).astype(jnp.bfloat16)
            for h in range(2):
                att[rows, cols[h]] = mixed[h * QB:(h + 1) * QB]
        else:
            m_ref[kept, :] = jnp.broadcast_to(top, (2 * QB, HD))
            l_ref[kept, :] = jnp.broadcast_to(total, (2 * QB, HD))
            acc_ref[kept, :] = mixed

    def attend(owner, parts, first, last):
        def step(b, carry):
            rows = pl.ds(pl.multiple_of(owner * tok + b * QB, QB), QB)
            if parts is None:
                picks = [(kv, t_smem[owner, b, e]) for e in range(ENTRIES)]
            else:
                base = z * cell + owner - lax.rem(b, 2) + n_seq
                picks = []
                for ref, layer in parts:
                    for r in range(cell // stride):
                        index = layer * cell + lax.rem(base, stride) + r * stride
                        e = lax.div(lax.rem(index - base + 2 * n_seq, n_seq), stride)
                        picks.append((ref, lax.rem(t_smem[owner, b, e], cell * nq)))
            for hh in range(hp):
                kcols = pl.ds(hh * HD, HD)
                keys = jnp.concatenate([ref[0, n, :, kcols] for ref, n in picks], 0)
                vals = jnp.concatenate([ref[1, n, :, kcols] for ref, n in picks], 0)
                for pair in range(gh // 2):
                    softmax_pass(keys, vals, rows, hh, pair, owner * nq + b, first, last)
            return carry

        lax.fori_loop(0, nq, step, 0)

    def attend_all(parts, first):
        def step(owner, carry):
            attend(owner, parts, first, False)
            return carry

        lax.fori_loop(0, cell, step, 0)

    def if_layer(layer):
        return pl.when(z == layer)

    def attend_last(owner):
        if not online:
            attend(owner, None, True, True)
            return
        for layer in range(Z):
            t = max(layer, Z - 1 - layer) - 1
            part = (kv_left[t], layer - 1 - t) if layer >= Z // 2 else (kv_right[t], layer + 1 + t)

            @if_layer(layer)
            def _(part=part):
                attend(owner, [part], False, True)

    def have_queries():
        for make in q_in:
            make().wait_recv()
        tcp = pltpu.make_async_copy(t_all, t_smem, local.at[5])
        tcp.start()
        tcp.wait()

    for cp in loc[:2]:
        cp.wait()
    for make in kv_in:
        make().wait_recv()
    for cond, make in kz(0)[0]:
        start_if(cond, make)
    send_rest()
    w_step(0)
    for cp in loc[2:]:
        cp.wait()
    if online:
        w_step(1)
        relay_y(1)
        w_step(2)
        k_step(0)
        relay_y(2)
        have_queries()
        for layer in range(Z):
            parts = [(kv, layer)]
            if layer > 0:
                parts.append((kv_left[0], layer - 1))
            if layer < Z - 1:
                parts.append((kv_right[0], layer + 1))

            @if_layer(layer)
            def _(parts=parts):
                attend_all(parts, True)

        relay_y()
        k_step(1)
        relay_x(4)
        for layer, part in ((0, (kv_right[1], 2)), (Z - 1, (kv_left[1], Z - 3))):

            @if_layer(layer)
            def _(part=part):
                attend_all([part], False)

        relay_x(5)
        k_step(2)
    else:
        for t in range(1, Z - 1):
            w_step(t)
        k_step(0)
        relay_y()
        for t in range(1, Z - 1):
            k_step(t)
        relay_x()
        have_queries()

    att_in = []
    for p in partners:
        attend_last(p)
        n = new_id()

        def make(n=n, p=p):
            return rcopy(n, att.at[pl.ds(pl.multiple_of(p * tok, 128), tok), :],
                         att_full.at[:, pl.ds(pl.multiple_of(i * qc, 128), qc)], g, z * cell + p)

        def landed(n=n, p=p):
            at = att_full.at[:, pl.ds(pl.multiple_of(p * qc, 128), qc)]
            return rcopy(n, at, at, g, z * cell + p)

        start(make)
        att_in.append(landed)
    relay_x()
    attend_last(i)
    own = pltpu.make_async_copy(att.at[pl.ds(pl.multiple_of(i * tok, 128), tok), :],
                                att_full.at[:, pl.ds(pl.multiple_of(i * qc, 128), qc)], local.at[6])
    own.start()
    own.wait()
    for make in att_in:
        make().wait_recv()
    for entry in final:
        maybe_wait(entry)

    for cond, make in pending:
        if cond is None:
            make().wait_send()
        else:
            @pl.when(cond)
            def _(make=make):
                make().wait_send()


def project(a_ref, w_ref, o_ref):
    o_ref[...] = jnp.dot(a_ref[...], w_ref[...], preferred_element_type=jnp.float32).astype(o_ref.dtype)


def body(Z, Y, queries, keys, values, block_table, out_weight):
    tok, width = queries.shape
    cell = 2 * Y
    hp = KVH // cell
    D = out_weight.shape[1]
    table = block_table
    online = Z == 4 and cell % (Z * cell // ENTRIES) == 0
    state = (cell * tok * H // KVH, HD) if online else (8, HD)
    blocks = (tok // QB, QB, KVH * HD)
    part = (2, cell * tok // QB, QB, hp * HD)
    steps = Z - 1
    n_sems = steps * 4 + (cell - 1) * 5 + 8 + steps * 2 * 9
    flops = 4 * tok * H * ENTRIES * QB * HD
    depth = out_weight.shape[0] * Z * cell
    attended, weight = pl.pallas_call(
        functools.partial(kernel, Z, Y, online),
        out_shape=(
            jax.ShapeDtypeStruct((tok, width), jnp.bfloat16),
            jax.ShapeDtypeStruct((depth, D), jnp.bfloat16),
        ),
        in_specs=[pl.BlockSpec(memory_space=pl.ANY)] * 5,
        out_specs=(pl.BlockSpec(memory_space=pl.ANY), pl.BlockSpec(memory_space=pl.ANY)),
        scratch_shapes=[
            pltpu.VMEM((cell * tok, width // cell), jnp.bfloat16),
            pltpu.VMEM(part if online else (2, Z * cell * tok // QB, QB, hp * HD), jnp.bfloat16),
            [pltpu.VMEM(part, jnp.bfloat16)] * (steps if online else 0),
            [pltpu.VMEM(part, jnp.bfloat16)] * (steps if online else 0),
            pltpu.VMEM((cell,) + table.shape, jnp.int32),
            pltpu.SMEM((cell,) + table.shape, jnp.int32),
            pltpu.VMEM((cell * tok, width // cell), jnp.bfloat16),
            pltpu.VMEM(state, jnp.float32),
            pltpu.VMEM(state, jnp.float32),
            pltpu.VMEM(state, jnp.float32),
            pltpu.SemaphoreType.DMA((n_sems,)),
            pltpu.SemaphoreType.DMA((n_sems,)),
            pltpu.SemaphoreType.DMA((7,)),
        ],
        compiler_params=pltpu.CompilerParams(
            collective_id=0, has_side_effects=True, vmem_limit_bytes=58 * 1024 * 1024,
        ),
        cost_estimate=pl.CostEstimate(flops=flops, bytes_accessed=64 * 1024 * 1024, transcendentals=0),
    )(queries, keys.reshape(blocks), values.reshape(blocks), table, out_weight)
    tile = 512
    return pl.pallas_call(
        project,
        grid=(D // tile,),
        out_shape=jax.ShapeDtypeStruct((tok, D), jnp.bfloat16),
        in_specs=[
            pl.BlockSpec((tok, depth), lambda j: (0, 0)),
            pl.BlockSpec((depth, tile), lambda j: (0, j)),
        ],
        out_specs=pl.BlockSpec((tok, tile), lambda j: (0, j)),
        compiler_params=pltpu.CompilerParams(vmem_limit_bytes=40 * 1024 * 1024),
        cost_estimate=pl.CostEstimate(
            flops=2 * tok * depth * D, bytes_accessed=2 * (tok * depth + depth * D + tok * D), transcendentals=0),
    )(attended, weight)


def solution(mesh):
    groups, seq = mesh.shape["groups"], mesh.shape["seq"]
    Y = 2 if groups == 2 else 1
    Z = seq // (2 * Y)
    in_specs = (
        P(("groups", "seq"), None),
        P(("groups", "seq"), None),
        P(("groups", "seq"), None),
        P(("groups", "seq"), None),
        P("seq", None),
    )
    return jax.shard_map(
        functools.partial(body, Z, Y), mesh=mesh, in_specs=in_specs,
        out_specs=P(("groups", "seq"), None), check_vma=False,
    )
```

```python
import functools

import jax
import jax.numpy as jnp
from jax import lax
from jax.experimental import pallas as pl
from jax.experimental.pallas import tpu as pltpu
from jax.sharding import PartitionSpec as P

H = 16
KVH = 4
HD = 128
QB = 128
ENTRIES = 8
MESH = pl.DeviceIdType.MESH
LOG2E = 1.4426950408889634


def kernel(
    Z, Y, online, q_ref, k_ref, v_ref, t_ref, w_ref, att_full, w_all,
    q_all, kv, kv_left, kv_right, t_all, t_smem, att, m_ref, l_ref, acc_ref, send, recv, local,
):
    cell = 2 * Y
    hp = KVH // cell
    gh = H // KVH
    tok = q_ref.shape[0]
    nq = tok // QB
    wrows = w_ref.shape[0]
    half = wrows // 2
    qc = hp * gh * HD
    kc = hp * HD

    g = lax.axis_index("groups")
    s = lax.axis_index("seq")
    z = lax.div(s, cell)
    i = lax.rem(s, cell)
    y = lax.div(i, 2)
    c = lax.rem(i, 2)
    xh = lax.rem(g, 2)
    gx = g + 1 - 2 * xh

    def dev(dy, dc):
        yy = 1 - y if dy else y
        cc = 1 - c if dc else c
        return yy * 2 + cc

    cores = i - c + (1 - c)
    partners = [dev(dy, dc) for dy in range(Y - 1, -1, -1) for dc in (1, 0) if dy or dc]
    has_left = z > 0
    has_right = z < Z - 1

    counter = [0]

    def new_id():
        counter[0] += 1
        return counter[0] - 1

    def rcopy(n, src, dst, gg, ss):
        return pltpu.make_async_remote_copy(
            src_ref=src, dst_ref=dst, send_sem=send.at[n], recv_sem=recv.at[n],
            device_id=(gg, ss), device_id_type=MESH,
        )

    pending = []

    barrier = pltpu.get_barrier_semaphore()
    for p in partners:
        pl.semaphore_signal(barrier, inc=1, device_id=(g, z * cell + p), device_id_type=MESH)
    pl.semaphore_signal(barrier, inc=1, device_id=(gx, s), device_id_type=MESH)

    @pl.when(has_left)
    def _():
        pl.semaphore_signal(barrier, inc=1, device_id=(g, s - cell), device_id_type=MESH)

    @pl.when(has_right)
    def _():
        pl.semaphore_signal(barrier, inc=1, device_id=(g, s + cell), device_id_type=MESH)

    edges = jnp.where(has_left, 1, 0) + jnp.where(has_right, 1, 0)
    pl.semaphore_wait(barrier, len(partners) + 1 + edges)

    def wunit(origin, idx, xx, rows=None):
        start = (origin * cell + idx) * wrows + xx * half
        return w_all.at[pl.ds(pl.multiple_of(start, 16), half), :]

    def wpair(origin, idx):
        start = (origin * cell + idx) * wrows
        return w_all.at[pl.ds(pl.multiple_of(start, 16), wrows), :]

    def layer_rows(origin):
        n = cell * nq
        return kv.at[:, pl.ds(origin * n, n)]

    def own_blocks(which, idx):
        return kv.at[which, pl.ds((idx if online else z * cell + idx) * nq, nq)]

    def z_copies(ids, src_of, dst_of, t):
        right = (has_right & (z - t >= 0), lambda: rcopy(ids[0], src_of(z - t), dst_of(z - t), g, s + cell))
        left = (has_left & (z + t <= Z - 1), lambda: rcopy(ids[1], src_of(z + t), dst_of(z + t), g, s - cell))
        from_left = (z - 1 - t >= 0, lambda: rcopy(ids[0], dst_of(z - 1 - t), dst_of(z - 1 - t), g, s + cell))
        from_right = (z + 1 + t <= Z - 1, lambda: rcopy(ids[1], dst_of(z + 1 + t), dst_of(z + 1 + t), g, s - cell))
        return (right, left), (from_left, from_right)

    def start_if(cond, make):
        @pl.when(cond)
        def _():
            make().start()

        pending.append((cond, make))

    def start(make):
        make().start()
        pending.append((None, make))

    def wait_recv_if(cond, make):
        @pl.when(cond)
        def _():
            make().wait_recv()

    loc = [
        pltpu.make_async_copy(k_ref.at[:, :, pl.ds(pl.multiple_of(i * kc, 128), kc)],
                              own_blocks(0, i), local.at[0]),
        pltpu.make_async_copy(v_ref.at[:, :, pl.ds(pl.multiple_of(i * kc, 128), kc)],
                              own_blocks(1, i), local.at[1]),
        pltpu.make_async_copy(q_ref.at[:, pl.ds(pl.multiple_of(i * qc, 128), qc)],
                              q_all.at[pl.ds(pl.multiple_of(i * tok, 128), tok), :], local.at[2]),
        pltpu.make_async_copy(t_ref, t_all.at[i], local.at[3]),
        pltpu.make_async_copy(w_ref, wpair(z, i), local.at[4]),
    ]
    for cp in loc:
        cp.start()

    def w_src0(origin):
        return w_ref.at[pl.ds(pl.multiple_of(xh * half, 16), half), :]

    wz_ids = [(new_id(), new_id()) for _ in range(Z - 1)]
    kz_ids = [(new_id(), new_id()) for _ in range(Z - 1)]

    def wz(t):
        if t == 0:
            dst = lambda origin: wunit(origin, i, xh)
            return z_copies(wz_ids[0], w_src0, dst, 0)
        same = lambda origin: wunit(origin, i, xh)
        return z_copies(wz_ids[t], same, same, t)

    def kz(t):
        if online:
            ids = kz_ids[t]
            to_right = lambda: rcopy(ids[0], kv_left[t - 1] if t else kv, kv_left[t], g, s + cell)
            to_left = lambda: rcopy(ids[1], kv_right[t - 1] if t else kv, kv_right[t], g, s - cell)
            right = (has_right & (z - t >= 0), to_right)
            left = (has_left & (z + t <= Z - 1), to_left)
            return (right, left), ((z - 1 - t >= 0, to_right), (z + 1 + t <= Z - 1, to_left))
        return z_copies(kz_ids[t], layer_rows, layer_rows, t)

    for cond, make in wz(0)[0]:
        start_if(cond, make)

    kv_in = []
    for p in partners:
        for which, ref in ((0, k_ref), (1, v_ref)):
            n = new_id()

            def make(n=n, p=p, which=which, ref=ref):
                return rcopy(n, ref.at[:, :, pl.ds(pl.multiple_of(p * kc, 128), kc)],
                             own_blocks(which, i), g, z * cell + p)

            def landed(n=n, p=p, which=which):
                at = own_blocks(which, p)
                return rcopy(n, at, at, g, z * cell + p)

            start(make)
            kv_in.append(landed)
    def w_send(make_src, make_dst, gg, ss, make_land, cond=None):
        n = new_id()
        make = lambda: rcopy(n, make_src(), make_dst(), gg, ss)
        if cond is None:
            start(make)
        else:
            start_if(cond, make)
        return (cond, lambda: rcopy(n, make_land(), make_land(), gg, ss))

    yi = (1 - y) * 2 + c
    core_dev = z * cell + cores
    y_dev = z * cell + yi
    y_cores = (1 - y) * 2 + (1 - c)

    def send_core(origin, idx, xx, idx_there, xx_there, cond=None):
        return w_send(lambda: wunit(origin, idx, xx), lambda: wunit(origin, idx, xx), g, core_dev,
                      lambda: wunit(origin, idx_there, xx_there), cond)

    final, y_lands, q_in = [], [], []

    def send_rest():
        n_own = new_id()
        own_core = lambda: rcopy(n_own, w_ref, wpair(z, i), g, core_dev)
        start(own_core)
        final.append((None, lambda: rcopy(n_own, wpair(z, cores), wpair(z, cores), g, core_dev)))
        if Y == 2:
            y_lands.append((z, None, w_send(lambda: w_src0(z), lambda: wunit(z, i, xh), g, y_dev,
                                            lambda: wunit(z, yi, xh))))
        for p in partners:
            n = new_id()

            def make(n=n, p=p):
                return rcopy(n, q_ref.at[:, pl.ds(pl.multiple_of(p * qc, 128), qc)],
                             q_all.at[pl.ds(pl.multiple_of(i * tok, 128), tok), :], g, z * cell + p)

            def landed(n=n, p=p):
                at = q_all.at[pl.ds(pl.multiple_of(p * tok, 128), tok), :]
                return rcopy(n, at, at, g, z * cell + p)

            start(make)
            q_in.append(landed)
            m = new_id()

            def make_t(m=m, p=p):
                return rcopy(m, t_ref, t_all.at[i], g, z * cell + p)

            def landed_t(m=m, p=p):
                return rcopy(m, t_all.at[p], t_all.at[p], g, z * cell + p)

            start(make_t)
            q_in.append(landed_t)


    x_lands = []

    def spread(origin, cond):
        x_lands.append((origin, cond, i, w_send(
            lambda: wunit(origin, i, xh), lambda: wunit(origin, i, xh), gx, s,
            lambda: wunit(origin, i, 1 - xh), cond)))
        if Y == 2:
            y_lands.append((origin, cond, w_send(
                lambda: wunit(origin, i, xh), lambda: wunit(origin, i, xh), g, y_dev,
                lambda: wunit(origin, yi, xh), cond)))
        final.append(send_core(origin, i, xh, cores, xh, cond))

    def maybe_wait(entry):
        cond, make = entry
        if cond is None:
            make().wait_recv()
        else:
            wait_recv_if(cond, make)

    def relay_y(count=1 << 20):
        while y_lands and count > 0:
            count -= 1
            origin, cond, entry = y_lands.pop(0)
            maybe_wait(entry)
            x_lands.append((origin, cond, yi, w_send(
                lambda origin=origin: wunit(origin, yi, xh), lambda origin=origin: wunit(origin, yi, xh), gx, s,
                lambda origin=origin: wunit(origin, yi, 1 - xh), cond)))
            final.append(send_core(origin, yi, xh, y_cores, xh, cond))

    def relay_x(count=1 << 20):
        while x_lands and count > 0:
            count -= 1
            origin, cond, idx, entry = x_lands.pop(0)
            maybe_wait(entry)
            there = cores if idx is i else y_cores
            final.append(send_core(origin, idx, 1 - xh, there, 1 - xh, cond))

    def w_step(t):
        for cond, make in wz(t)[1]:
            wait_recv_if(cond, make)
        if t + 1 < Z - 1:
            for cond, make in wz(t + 1)[0]:
                start_if(cond, make)
        spread(z - 1 - t, z - 1 - t >= 0)
        spread(z + 1 + t, z + 1 + t <= Z - 1)

    def k_step(t):
        for cond, make in kz(t)[1]:
            wait_recv_if(cond, make)
        if t + 1 < Z - 1:
            for cond, make in kz(t + 1)[0]:
                start_if(cond, make)

    factor = HD ** -0.5 * LOG2E
    n_seq = Z * cell
    stride = n_seq // ENTRIES

    def softmax_pass(keys, vals, rows, hh, block, first, last):
        cols = [pl.ds((hh * gh + h) * HD, HD) for h in range(gh)]
        qq = jnp.concatenate([q_all[rows, cc] for cc in cols], 0)
        sc = lax.dot_general(keys, qq, (((1,), (1,)), ((), ())), preferred_element_type=jnp.float32)
        top = jnp.max(sc, axis=0, keepdims=True)
        if not first:
            before = m_ref[block]
            top = jnp.maximum(before, top)
        wts = jnp.exp2((sc - top) * factor)
        total = jnp.sum(wts, axis=0, keepdims=True)
        mixed = lax.dot_general(vals, wts.astype(jnp.bfloat16), (((0,), (0,)), ((), ())),
                                preferred_element_type=jnp.float32)
        if not first:
            shrink = jnp.exp2((before - top) * factor)
            total = total + l_ref[block] * shrink
            mixed = mixed + acc_ref[block] * shrink
        if last:
            mixed = mixed / total
            for h in range(gh):
                att[rows, cols[h]] = mixed[:, h * QB:(h + 1) * QB].T.astype(jnp.bfloat16)
        else:
            m_ref[block] = top
            l_ref[block] = total
            acc_ref[block] = mixed

    def attend(owner, parts, first, last):
        def step(b, carry):
            rows = pl.ds(pl.multiple_of(owner * tok + b * QB, QB), QB)
            if parts is None:
                picks = [(kv, t_smem[owner, b, e]) for e in range(ENTRIES)]
            else:
                base = z * cell + owner - lax.rem(b, 2) + n_seq
                picks = []
                for ref, layer in parts:
                    for r in range(cell // stride):
                        index = layer * cell + lax.rem(base, stride) + r * stride
                        e = lax.div(lax.rem(index - base + 2 * n_seq, n_seq), stride)
                        picks.append((ref, lax.rem(t_smem[owner, b, e], cell * nq)))
            for hh in range(hp):
                kcols = pl.ds(hh * HD, HD)
                keys = jnp.concatenate([ref[0, n, :, kcols] for ref, n in picks], 0)
                vals = jnp.concatenate([ref[1, n, :, kcols] for ref, n in picks], 0)
                softmax_pass(keys, vals, rows, hh, owner * nq + b, first, last)
            return carry

        lax.fori_loop(0, nq, step, 0)

    def attend_all(parts, first):
        def step(owner, carry):
            attend(owner, parts, first, False)
            return carry

        lax.fori_loop(0, cell, step, 0)

    def if_layer(layer):
        return pl.when(z == layer)

    def attend_last(owner):
        if not online:
            attend(owner, None, True, True)
            return
        for layer in range(Z):
            near = first_parts(layer)
            parts = [part for part in brought(layer) if part[1] not in [p[1] for p in near]]
            if layer in (0, Z - 1):
                parts = parts[-1:]

            @if_layer(layer)
            def _(parts=parts):
                attend(owner, parts, False, True)

    def brought(layer):
        parts = []
        for t in range(Z - 1):
            if layer - 1 - t >= 0:
                parts.append((kv_left[t], layer - 1 - t))
            if layer + 1 + t < Z:
                parts.append((kv_right[t], layer + 1 + t))
        return parts

    def first_parts(layer):
        return [(kv, layer), brought(layer)[0]]

    def have_queries():
        for make in q_in:
            make().wait_recv()
        tcp = pltpu.make_async_copy(t_all, t_smem, local.at[5])
        tcp.start()
        tcp.wait()

    for cp in loc[:2]:
        cp.wait()
    for make in kv_in:
        make().wait_recv()
    for cond, make in kz(0)[0]:
        start_if(cond, make)
    send_rest()
    w_step(0)
    for cp in loc[2:]:
        cp.wait()
    if online:
        w_step(1)
        relay_y(1)
        w_step(2)
        k_step(0)
        relay_y(2)
        have_queries()
        for layer in range(Z):
            parts = first_parts(layer)

            @if_layer(layer)
            def _(parts=parts):
                attend_all(parts, True)

        k_step(1)
        relay_y()
        relay_x(5)
        for layer, part in ((0, (kv_right[1], 2)), (Z - 1, (kv_left[1], Z - 3))):

            @if_layer(layer)
            def _(part=part):
                attend_all([part], False)

        relay_x(4)
        k_step(2)
    else:
        for t in range(1, Z - 1):
            w_step(t)
        k_step(0)
        relay_y()
        for t in range(1, Z - 1):
            k_step(t)
        relay_x()
        have_queries()

    att_in = []
    for p in partners:
        attend_last(p)
        n = new_id()

        def make(n=n, p=p):
            return rcopy(n, att.at[pl.ds(pl.multiple_of(p * tok, 128), tok), :],
                         att_full.at[:, pl.ds(pl.multiple_of(i * qc, 128), qc)], g, z * cell + p)

        def landed(n=n, p=p):
            at = att_full.at[:, pl.ds(pl.multiple_of(p * qc, 128), qc)]
            return rcopy(n, at, at, g, z * cell + p)

        start(make)
        att_in.append(landed)
    relay_x()
    attend_last(i)
    own = pltpu.make_async_copy(att.at[pl.ds(pl.multiple_of(i * tok, 128), tok), :],
                                att_full.at[:, pl.ds(pl.multiple_of(i * qc, 128), qc)], local.at[6])
    own.start()
    own.wait()
    for make in att_in:
        make().wait_recv()
    for entry in final:
        maybe_wait(entry)

    for cond, make in pending:
        if cond is None:
            make().wait_send()
        else:
            @pl.when(cond)
            def _(make=make):
                make().wait_send()


def project(a_ref, w_ref, o_ref):
    o_ref[...] = jnp.dot(a_ref[...], w_ref[...], preferred_element_type=jnp.float32).astype(o_ref.dtype)


def body(Z, Y, queries, keys, values, block_table, out_weight):
    tok, width = queries.shape
    cell = 2 * Y
    hp = KVH // cell
    D = out_weight.shape[1]
    table = block_table
    online = Z == 4 and cell % (Z * cell // ENTRIES) == 0
    blocks_here = cell * tok // QB if online else 1
    rows = H // KVH * QB
    blocks = (tok // QB, QB, KVH * HD)
    part = (2, cell * tok // QB, QB, hp * HD)
    steps = Z - 1
    n_sems = steps * 4 + (cell - 1) * 5 + 8 + steps * 2 * 9
    flops = 4 * tok * H * ENTRIES * QB * HD
    depth = out_weight.shape[0] * Z * cell
    attended, weight = pl.pallas_call(
        functools.partial(kernel, Z, Y, online),
        out_shape=(
            jax.ShapeDtypeStruct((tok, width), jnp.bfloat16),
            jax.ShapeDtypeStruct((depth, D), jnp.bfloat16),
        ),
        in_specs=[pl.BlockSpec(memory_space=pl.ANY)] * 5,
        out_specs=(pl.BlockSpec(memory_space=pl.ANY), pl.BlockSpec(memory_space=pl.ANY)),
        scratch_shapes=[
            pltpu.VMEM((cell * tok, width // cell), jnp.bfloat16),
            pltpu.VMEM(part if online else (2, Z * cell * tok // QB, QB, hp * HD), jnp.bfloat16),
            [pltpu.VMEM(part, jnp.bfloat16)] * (steps if online else 0),
            [pltpu.VMEM(part, jnp.bfloat16)] * (steps if online else 0),
            pltpu.VMEM((cell,) + table.shape, jnp.int32),
            pltpu.SMEM((cell,) + table.shape, jnp.int32),
            pltpu.VMEM((cell * tok, width // cell), jnp.bfloat16),
            pltpu.VMEM((blocks_here, 1, rows), jnp.float32),
            pltpu.VMEM((blocks_here, 1, rows), jnp.float32),
            pltpu.VMEM((blocks_here, HD, rows), jnp.float32),
            pltpu.SemaphoreType.DMA((n_sems,)),
            pltpu.SemaphoreType.DMA((n_sems,)),
            pltpu.SemaphoreType.DMA((7,)),
        ],
        compiler_params=pltpu.CompilerParams(
            collective_id=0, has_side_effects=True, vmem_limit_bytes=58 * 1024 * 1024,
        ),
        cost_estimate=pl.CostEstimate(flops=flops, bytes_accessed=64 * 1024 * 1024, transcendentals=0),
    )(queries, keys.reshape(blocks), values.reshape(blocks), table, out_weight)
    tile = 512
    return pl.pallas_call(
        project,
        grid=(D // tile,),
        out_shape=jax.ShapeDtypeStruct((tok, D), jnp.bfloat16),
        in_specs=[
            pl.BlockSpec((tok, depth), lambda j: (0, 0)),
            pl.BlockSpec((depth, tile), lambda j: (0, j)),
        ],
        out_specs=pl.BlockSpec((tok, tile), lambda j: (0, j)),
        compiler_params=pltpu.CompilerParams(vmem_limit_bytes=60 * 1024 * 1024),
        cost_estimate=pl.CostEstimate(
            flops=2 * tok * depth * D, bytes_accessed=2 * (tok * depth + depth * D + tok * D), transcendentals=0),
    )(attended, weight)


def solution(mesh):
    groups, seq = mesh.shape["groups"], mesh.shape["seq"]
    Y = 2 if groups == 2 else 1
    Z = seq // (2 * Y)
    in_specs = (
        P(("groups", "seq"), None),
        P(("groups", "seq"), None),
        P(("groups", "seq"), None),
        P(("groups", "seq"), None),
        P("seq", None),
    )
    return jax.shard_map(
        functools.partial(body, Z, Y), mesh=mesh, in_specs=in_specs,
        out_specs=P(("groups", "seq"), None), check_vma=False,
    )
```

```python
import functools

import jax
import jax.numpy as jnp
from jax import lax
from jax.experimental import pallas as pl
from jax.experimental.pallas import tpu as pltpu
from jax.sharding import PartitionSpec as P

H = 16
KVH = 4
HD = 128
QB = 128
ENTRIES = 8
MESH = pl.DeviceIdType.MESH
LOG2E = 1.4426950408889634


def kernel(
    Z, Y, online, q_ref, k_ref, v_ref, t_ref, w_ref, att_full, w_all,
    q_all, kv, kv_left, kv_right, t_all, t_smem, att, m_ref, l_ref, acc_ref, send, recv, local,
):
    cell = 2 * Y
    hp = KVH // cell
    gh = H // KVH
    tok = q_ref.shape[0]
    nq = tok // QB
    wrows = w_ref.shape[0]
    half = wrows // 2
    qc = hp * gh * HD
    kc = hp * HD

    g = lax.axis_index("groups")
    s = lax.axis_index("seq")
    z = lax.div(s, cell)
    i = lax.rem(s, cell)
    y = lax.div(i, 2)
    c = lax.rem(i, 2)
    xh = lax.rem(g, 2)
    gx = g + 1 - 2 * xh

    def dev(dy, dc):
        yy = 1 - y if dy else y
        cc = 1 - c if dc else c
        return yy * 2 + cc

    cores = i - c + (1 - c)
    partners = [dev(dy, dc) for dy in range(Y - 1, -1, -1) for dc in (1, 0) if dy or dc]
    has_left = z > 0
    has_right = z < Z - 1

    counter = [0]

    def new_id():
        counter[0] += 1
        return counter[0] - 1

    def rcopy(n, src, dst, gg, ss):
        return pltpu.make_async_remote_copy(
            src_ref=src, dst_ref=dst, send_sem=send.at[n], recv_sem=recv.at[n],
            device_id=(gg, ss), device_id_type=MESH,
        )

    pending = []

    barrier = pltpu.get_barrier_semaphore()
    for p in partners:
        pl.semaphore_signal(barrier, inc=1, device_id=(g, z * cell + p), device_id_type=MESH)
    pl.semaphore_signal(barrier, inc=1, device_id=(gx, s), device_id_type=MESH)

    @pl.when(has_left)
    def _():
        pl.semaphore_signal(barrier, inc=1, device_id=(g, s - cell), device_id_type=MESH)

    @pl.when(has_right)
    def _():
        pl.semaphore_signal(barrier, inc=1, device_id=(g, s + cell), device_id_type=MESH)

    edges = jnp.where(has_left, 1, 0) + jnp.where(has_right, 1, 0)
    pl.semaphore_wait(barrier, len(partners) + 1 + edges)

    def wunit(origin, idx, xx, rows=None):
        start = (origin * cell + idx) * wrows + xx * half
        return w_all.at[pl.ds(pl.multiple_of(start, 16), half), :]

    def wpair(origin, idx):
        start = (origin * cell + idx) * wrows
        return w_all.at[pl.ds(pl.multiple_of(start, 16), wrows), :]

    def layer_rows(origin):
        n = cell * nq
        return kv.at[:, pl.ds(origin * n, n)]

    def own_blocks(which, idx):
        return kv.at[which, pl.ds((idx if online else z * cell + idx) * nq, nq)]

    def z_copies(ids, src_of, dst_of, t):
        right = (has_right & (z - t >= 0), lambda: rcopy(ids[0], src_of(z - t), dst_of(z - t), g, s + cell))
        left = (has_left & (z + t <= Z - 1), lambda: rcopy(ids[1], src_of(z + t), dst_of(z + t), g, s - cell))
        from_left = (z - 1 - t >= 0, lambda: rcopy(ids[0], dst_of(z - 1 - t), dst_of(z - 1 - t), g, s + cell))
        from_right = (z + 1 + t <= Z - 1, lambda: rcopy(ids[1], dst_of(z + 1 + t), dst_of(z + 1 + t), g, s - cell))
        return (right, left), (from_left, from_right)

    def start_if(cond, make):
        @pl.when(cond)
        def _():
            make().start()

        pending.append((cond, make))

    def start(make):
        make().start()
        pending.append((None, make))

    def wait_recv_if(cond, make):
        @pl.when(cond)
        def _():
            make().wait_recv()

    loc = [
        pltpu.make_async_copy(k_ref.at[:, :, pl.ds(pl.multiple_of(i * kc, 128), kc)],
                              own_blocks(0, i), local.at[0]),
        pltpu.make_async_copy(v_ref.at[:, :, pl.ds(pl.multiple_of(i * kc, 128), kc)],
                              own_blocks(1, i), local.at[1]),
        pltpu.make_async_copy(q_ref.at[:, pl.ds(pl.multiple_of(i * qc, 128), qc)],
                              q_all.at[pl.ds(pl.multiple_of(i * tok, 128), tok), :], local.at[2]),
        pltpu.make_async_copy(t_ref, t_all.at[i], local.at[3]),
        pltpu.make_async_copy(w_ref, wpair(z, i), local.at[4]),
    ]
    for cp in loc:
        cp.start()

    def w_src0(origin):
        return w_ref.at[pl.ds(pl.multiple_of(xh * half, 16), half), :]

    wz_ids = [(new_id(), new_id()) for _ in range(Z - 1)]
    kz_ids = [(new_id(), new_id()) for _ in range(Z - 1)]

    def wz(t):
        if t == 0:
            dst = lambda origin: wunit(origin, i, xh)
            return z_copies(wz_ids[0], w_src0, dst, 0)
        same = lambda origin: wunit(origin, i, xh)
        return z_copies(wz_ids[t], same, same, t)

    def kz(t):
        if online:
            ids = kz_ids[t]
            to_right = lambda: rcopy(ids[0], kv_left[t - 1] if t else kv, kv_left[t], g, s + cell)
            to_left = lambda: rcopy(ids[1], kv_right[t - 1] if t else kv, kv_right[t], g, s - cell)
            right = (has_right & (z - t >= 0), to_right)
            left = (has_left & (z + t <= Z - 1), to_left)
            return (right, left), ((z - 1 - t >= 0, to_right), (z + 1 + t <= Z - 1, to_left))
        return z_copies(kz_ids[t], layer_rows, layer_rows, t)

    for cond, make in wz(0)[0]:
        start_if(cond, make)

    kv_in = []
    for p in partners:
        for which, ref in ((0, k_ref), (1, v_ref)):
            n = new_id()

            def make(n=n, p=p, which=which, ref=ref):
                return rcopy(n, ref.at[:, :, pl.ds(pl.multiple_of(p * kc, 128), kc)],
                             own_blocks(which, i), g, z * cell + p)

            def landed(n=n, p=p, which=which):
                at = own_blocks(which, p)
                return rcopy(n, at, at, g, z * cell + p)

            start(make)
            kv_in.append(landed)
    def w_send(make_src, make_dst, gg, ss, make_land, cond=None):
        n = new_id()
        make = lambda: rcopy(n, make_src(), make_dst(), gg, ss)
        if cond is None:
            start(make)
        else:
            start_if(cond, make)
        return (cond, lambda: rcopy(n, make_land(), make_land(), gg, ss))

    yi = (1 - y) * 2 + c
    core_dev = z * cell + cores
    y_dev = z * cell + yi
    y_cores = (1 - y) * 2 + (1 - c)

    def send_core(origin, idx, xx, idx_there, xx_there, cond=None):
        return w_send(lambda: wunit(origin, idx, xx), lambda: wunit(origin, idx, xx), g, core_dev,
                      lambda: wunit(origin, idx_there, xx_there), cond)

    final, y_lands, q_in = [], [], []

    def send_own_weight():
        n_own = new_id()
        own_core = lambda: rcopy(n_own, w_ref, wpair(z, i), g, core_dev)
        start(own_core)
        final.append((None, lambda: rcopy(n_own, wpair(z, cores), wpair(z, cores), g, core_dev)))
        if Y == 2:
            y_lands.append((z, None, w_send(lambda: w_src0(z), lambda: wunit(z, i, xh), g, y_dev,
                                            lambda: wunit(z, yi, xh))))

    def send_queries():
        for p in partners:
            n = new_id()

            def make(n=n, p=p):
                return rcopy(n, q_ref.at[:, pl.ds(pl.multiple_of(p * qc, 128), qc)],
                             q_all.at[pl.ds(pl.multiple_of(i * tok, 128), tok), :], g, z * cell + p)

            def landed(n=n, p=p):
                at = q_all.at[pl.ds(pl.multiple_of(p * tok, 128), tok), :]
                return rcopy(n, at, at, g, z * cell + p)

            start(make)
            q_in.append(landed)
            m = new_id()

            def make_t(m=m, p=p):
                return rcopy(m, t_ref, t_all.at[i], g, z * cell + p)

            def landed_t(m=m, p=p):
                return rcopy(m, t_all.at[p], t_all.at[p], g, z * cell + p)

            start(make_t)
            q_in.append(landed_t)


    x_lands = []

    def spread(origin, cond):
        x_lands.append((origin, cond, i, w_send(
            lambda: wunit(origin, i, xh), lambda: wunit(origin, i, xh), gx, s,
            lambda: wunit(origin, i, 1 - xh), cond)))
        if Y == 2:
            y_lands.append((origin, cond, w_send(
                lambda: wunit(origin, i, xh), lambda: wunit(origin, i, xh), g, y_dev,
                lambda: wunit(origin, yi, xh), cond)))
        final.append(send_core(origin, i, xh, cores, xh, cond))

    def maybe_wait(entry):
        cond, make = entry
        if cond is None:
            make().wait_recv()
        else:
            wait_recv_if(cond, make)

    def relay_y(count=1 << 20):
        while y_lands and count > 0:
            count -= 1
            origin, cond, entry = y_lands.pop(0)
            maybe_wait(entry)
            x_lands.append((origin, cond, yi, w_send(
                lambda origin=origin: wunit(origin, yi, xh), lambda origin=origin: wunit(origin, yi, xh), gx, s,
                lambda origin=origin: wunit(origin, yi, 1 - xh), cond)))
            final.append(send_core(origin, yi, xh, y_cores, xh, cond))

    def relay_x(count=1 << 20):
        while x_lands and count > 0:
            count -= 1
            origin, cond, idx, entry = x_lands.pop(0)
            maybe_wait(entry)
            there = cores if idx is i else y_cores
            final.append(send_core(origin, idx, 1 - xh, there, 1 - xh, cond))

    def w_step(t):
        for cond, make in wz(t)[1]:
            wait_recv_if(cond, make)
        if t + 1 < Z - 1:
            for cond, make in wz(t + 1)[0]:
                start_if(cond, make)
        spread(z - 1 - t, z - 1 - t >= 0)
        spread(z + 1 + t, z + 1 + t <= Z - 1)

    def k_step(t):
        for cond, make in kz(t)[1]:
            wait_recv_if(cond, make)
        if t + 1 < Z - 1:
            for cond, make in kz(t + 1)[0]:
                start_if(cond, make)

    factor = HD ** -0.5 * LOG2E
    n_seq = Z * cell
    stride = n_seq // ENTRIES

    def softmax_pass(keys, vals, rows, hh, block, first, last):
        cols = [pl.ds((hh * gh + h) * HD, HD) for h in range(gh)]
        qq = jnp.concatenate([q_all[rows, cc] for cc in cols], 0)
        sc = lax.dot_general(keys, qq, (((1,), (1,)), ((), ())), preferred_element_type=jnp.float32)
        top = jnp.max(sc, axis=0, keepdims=True)
        if not first:
            before = m_ref[block]
            top = jnp.maximum(before, top)
        wts = jnp.exp2((sc - top) * factor)
        total = jnp.sum(wts, axis=0, keepdims=True)
        mixed = lax.dot_general(vals, wts.astype(jnp.bfloat16), (((0,), (0,)), ((), ())),
                                preferred_element_type=jnp.float32)
        if not first:
            shrink = jnp.exp2((before - top) * factor)
            total = total + l_ref[block] * shrink
            mixed = mixed + acc_ref[block] * shrink
        if last:
            mixed = mixed / total
            for h in range(gh):
                att[rows, cols[h]] = mixed[:, h * QB:(h + 1) * QB].T.astype(jnp.bfloat16)
        else:
            m_ref[block] = top
            l_ref[block] = total
            acc_ref[block] = mixed

    def attend(owner, parts, first, last):
        def step(b, carry):
            rows = pl.ds(pl.multiple_of(owner * tok + b * QB, QB), QB)
            if parts is None:
                picks = [(kv, t_smem[owner, b, e]) for e in range(ENTRIES)]
            else:
                base = z * cell + owner - lax.rem(b, 2) + n_seq
                picks = []
                for ref, layer in parts:
                    for r in range(cell // stride):
                        index = layer * cell + lax.rem(base, stride) + r * stride
                        e = lax.div(lax.rem(index - base + 2 * n_seq, n_seq), stride)
                        picks.append((ref, lax.rem(t_smem[owner, b, e], cell * nq)))
            for hh in range(hp):
                kcols = pl.ds(hh * HD, HD)
                keys = jnp.concatenate([ref[0, n, :, kcols] for ref, n in picks], 0)
                vals = jnp.concatenate([ref[1, n, :, kcols] for ref, n in picks], 0)
                softmax_pass(keys, vals, rows, hh, owner * nq + b, first, last)
            return carry

        lax.fori_loop(0, nq, step, 0)

    def attend_all(parts, first):
        def step(owner, carry):
            attend(owner, parts, first, False)
            return carry

        lax.fori_loop(0, cell, step, 0)

    def if_layer(layer):
        return pl.when(z == layer)

    def attend_last(owner):
        if not online:
            attend(owner, None, True, True)
            return
        for layer in range(Z):
            parts = brought(layer)[-1:]

            @if_layer(layer)
            def _(parts=parts):
                attend(owner, parts, False, True)

    def brought(layer):
        parts = []
        for t in range(Z - 1):
            if layer - 1 - t >= 0:
                parts.append((kv_left[t], layer - 1 - t))
            if layer + 1 + t < Z:
                parts.append((kv_right[t], layer + 1 + t))
        return parts

    def have_queries():
        for make in q_in:
            make().wait_recv()
        tcp = pltpu.make_async_copy(t_all, t_smem, local.at[5])
        tcp.start()
        tcp.wait()

    def start_keys():
        for cp in loc:
            cp.wait()
        for make in kv_in:
            make().wait_recv()
        for cond, make in kz(0)[0]:
            start_if(cond, make)

    send_own_weight()
    w_step(0)
    if online:
        w_step(1)
        start_keys()
        relay_y(3)
        w_step(2)
        relay_y(2)
        k_step(0)
        relay_y()
        send_queries()
        relay_x(4)
        k_step(1)
        have_queries()
        for layer in range(Z):
            parts = [(kv, layer)] + brought(layer)[:-1]

            @if_layer(layer)
            def _(parts=parts):
                attend_all(parts, True)

        relay_x()
        k_step(2)
    else:
        start_keys()
        send_queries()
        for t in range(1, Z - 1):
            w_step(t)
        k_step(0)
        relay_y()
        for t in range(1, Z - 1):
            k_step(t)
        relay_x()
        have_queries()

    att_in = []
    for p in partners:
        attend_last(p)
        n = new_id()

        def make(n=n, p=p):
            return rcopy(n, att.at[pl.ds(pl.multiple_of(p * tok, 128), tok), :],
                         att_full.at[:, pl.ds(pl.multiple_of(i * qc, 128), qc)], g, z * cell + p)

        def landed(n=n, p=p):
            at = att_full.at[:, pl.ds(pl.multiple_of(p * qc, 128), qc)]
            return rcopy(n, at, at, g, z * cell + p)

        start(make)
        att_in.append(landed)
    relay_x()
    attend_last(i)
    own = pltpu.make_async_copy(att.at[pl.ds(pl.multiple_of(i * tok, 128), tok), :],
                                att_full.at[:, pl.ds(pl.multiple_of(i * qc, 128), qc)], local.at[6])
    own.start()
    own.wait()
    for make in att_in:
        make().wait_recv()
    for entry in final:
        maybe_wait(entry)

    for cond, make in pending:
        if cond is None:
            make().wait_send()
        else:
            @pl.when(cond)
            def _(make=make):
                make().wait_send()


def project(a_ref, w_ref, o_ref):
    o_ref[...] = jnp.dot(a_ref[...], w_ref[...], preferred_element_type=jnp.float32).astype(o_ref.dtype)


def body(Z, Y, queries, keys, values, block_table, out_weight):
    tok, width = queries.shape
    cell = 2 * Y
    hp = KVH // cell
    D = out_weight.shape[1]
    table = block_table
    online = Z == 4 and cell % (Z * cell // ENTRIES) == 0
    blocks_here = cell * tok // QB if online else 1
    rows = H // KVH * QB
    blocks = (tok // QB, QB, KVH * HD)
    part = (2, cell * tok // QB, QB, hp * HD)
    steps = Z - 1
    n_sems = steps * 4 + (cell - 1) * 5 + 8 + steps * 2 * 9
    flops = 4 * tok * H * ENTRIES * QB * HD
    depth = out_weight.shape[0] * Z * cell
    attended, weight = pl.pallas_call(
        functools.partial(kernel, Z, Y, online),
        out_shape=(
            jax.ShapeDtypeStruct((tok, width), jnp.bfloat16),
            jax.ShapeDtypeStruct((depth, D), jnp.bfloat16),
        ),
        in_specs=[pl.BlockSpec(memory_space=pl.ANY)] * 5,
        out_specs=(pl.BlockSpec(memory_space=pl.ANY), pl.BlockSpec(memory_space=pl.ANY)),
        scratch_shapes=[
            pltpu.VMEM((cell * tok, width // cell), jnp.bfloat16),
            pltpu.VMEM(part if online else (2, Z * cell * tok // QB, QB, hp * HD), jnp.bfloat16),
            [pltpu.VMEM(part, jnp.bfloat16)] * (steps if online else 0),
            [pltpu.VMEM(part, jnp.bfloat16)] * (steps if online else 0),
            pltpu.VMEM((cell,) + table.shape, jnp.int32),
            pltpu.SMEM((cell,) + table.shape, jnp.int32),
            pltpu.VMEM((cell * tok, width // cell), jnp.bfloat16),
            pltpu.VMEM((blocks_here, 1, rows), jnp.float32),
            pltpu.VMEM((blocks_here, 1, rows), jnp.float32),
            pltpu.VMEM((blocks_here, HD, rows), jnp.float32),
            pltpu.SemaphoreType.DMA((n_sems,)),
            pltpu.SemaphoreType.DMA((n_sems,)),
            pltpu.SemaphoreType.DMA((7,)),
        ],
        compiler_params=pltpu.CompilerParams(
            collective_id=0, has_side_effects=True, vmem_limit_bytes=58 * 1024 * 1024,
        ),
        cost_estimate=pl.CostEstimate(flops=flops, bytes_accessed=64 * 1024 * 1024, transcendentals=0),
    )(queries, keys.reshape(blocks), values.reshape(blocks), table, out_weight)
    tile = 512
    return pl.pallas_call(
        project,
        grid=(D // tile,),
        out_shape=jax.ShapeDtypeStruct((tok, D), jnp.bfloat16),
        in_specs=[
            pl.BlockSpec((tok, depth), lambda j: (0, 0)),
            pl.BlockSpec((depth, tile), lambda j: (0, j)),
        ],
        out_specs=pl.BlockSpec((tok, tile), lambda j: (0, j)),
        compiler_params=pltpu.CompilerParams(vmem_limit_bytes=60 * 1024 * 1024),
        cost_estimate=pl.CostEstimate(
            flops=2 * tok * depth * D, bytes_accessed=2 * (tok * depth + depth * D + tok * D), transcendentals=0),
    )(attended, weight)


def solution(mesh):
    groups, seq = mesh.shape["groups"], mesh.shape["seq"]
    Y = 2 if groups == 2 else 1
    Z = seq // (2 * Y)
    in_specs = (
        P(("groups", "seq"), None),
        P(("groups", "seq"), None),
        P(("groups", "seq"), None),
        P(("groups", "seq"), None),
        P("seq", None),
    )
    return jax.shard_map(
        functools.partial(body, Z, Y), mesh=mesh, in_specs=in_specs,
        out_specs=P(("groups", "seq"), None), check_vma=False,
    )
```

```python
import functools

import jax
import jax.numpy as jnp
from jax import lax
from jax.experimental import pallas as pl
from jax.experimental.pallas import tpu as pltpu
from jax.sharding import PartitionSpec as P

H = 16
KVH = 4
HD = 128
QB = 128
ENTRIES = 8
MESH = pl.DeviceIdType.MESH
LOG2E = 1.4426950408889634


def kernel(
    Z, Y, online, q_ref, k_ref, v_ref, t_ref, w_ref, att_full, w_all,
    q_all, kv, kv_left, kv_right, t_all, t_smem, att, m_ref, l_ref, acc_ref, send, recv, local,
):
    cell = 2 * Y
    hp = KVH // cell
    gh = H // KVH
    tok = q_ref.shape[0]
    nq = tok // QB
    wrows = w_ref.shape[0]
    half = wrows // 2
    qc = hp * gh * HD
    kc = hp * HD

    g = lax.axis_index("groups")
    s = lax.axis_index("seq")
    z = lax.div(s, cell)
    i = lax.rem(s, cell)
    y = lax.div(i, 2)
    c = lax.rem(i, 2)
    xh = lax.rem(g, 2)
    gx = g + 1 - 2 * xh

    def dev(dy, dc):
        yy = 1 - y if dy else y
        cc = 1 - c if dc else c
        return yy * 2 + cc

    cores = i - c + (1 - c)
    partners = [dev(dy, dc) for dy in range(Y - 1, -1, -1) for dc in (1, 0) if dy or dc]
    has_left = z > 0
    has_right = z < Z - 1

    counter = [0]

    def new_id():
        counter[0] += 1
        return counter[0] - 1

    def rcopy(n, src, dst, gg, ss):
        return pltpu.make_async_remote_copy(
            src_ref=src, dst_ref=dst, send_sem=send.at[n], recv_sem=recv.at[n],
            device_id=(gg, ss), device_id_type=MESH,
        )

    pending = []

    barrier = pltpu.get_barrier_semaphore()
    for p in partners:
        pl.semaphore_signal(barrier, inc=1, device_id=(g, z * cell + p), device_id_type=MESH)
    pl.semaphore_signal(barrier, inc=1, device_id=(gx, s), device_id_type=MESH)

    @pl.when(has_left)
    def _():
        pl.semaphore_signal(barrier, inc=1, device_id=(g, s - cell), device_id_type=MESH)

    @pl.when(has_right)
    def _():
        pl.semaphore_signal(barrier, inc=1, device_id=(g, s + cell), device_id_type=MESH)

    edges = jnp.where(has_left, 1, 0) + jnp.where(has_right, 1, 0)
    pl.semaphore_wait(barrier, len(partners) + 1 + edges)

    def wunit(origin, idx, xx, rows=None):
        start = (origin * cell + idx) * wrows + xx * half
        return w_all.at[pl.ds(pl.multiple_of(start, 16), half), :]

    def wpair(origin, idx):
        start = (origin * cell + idx) * wrows
        return w_all.at[pl.ds(pl.multiple_of(start, 16), wrows), :]

    def layer_rows(origin, a):
        n = cell * nq
        return kv.at[a, pl.ds(origin * n, n)]

    def own_blocks(which, idx):
        return kv.at[which, pl.ds((idx if online else z * cell + idx) * nq, nq)]

    def z_copies(ids, src_of, dst_of, t):
        right = (has_right & (z - t >= 0), lambda: rcopy(ids[0], src_of(z - t), dst_of(z - t), g, s + cell))
        left = (has_left & (z + t <= Z - 1), lambda: rcopy(ids[1], src_of(z + t), dst_of(z + t), g, s - cell))
        from_left = (z - 1 - t >= 0, lambda: rcopy(ids[0], dst_of(z - 1 - t), dst_of(z - 1 - t), g, s + cell))
        from_right = (z + 1 + t <= Z - 1, lambda: rcopy(ids[1], dst_of(z + 1 + t), dst_of(z + 1 + t), g, s - cell))
        return (right, left), (from_left, from_right)

    def start_if(cond, make):
        @pl.when(cond)
        def _():
            make().start()

        pending.append((cond, make))

    def start(make):
        make().start()
        pending.append((None, make))

    def wait_recv_if(cond, make):
        @pl.when(cond)
        def _():
            make().wait_recv()

    loc = [
        pltpu.make_async_copy(k_ref.at[:, :, pl.ds(pl.multiple_of(i * kc, 128), kc)],
                              own_blocks(0, i), local.at[0]),
        pltpu.make_async_copy(v_ref.at[:, :, pl.ds(pl.multiple_of(i * kc, 128), kc)],
                              own_blocks(1, i), local.at[1]),
        pltpu.make_async_copy(q_ref.at[:, pl.ds(pl.multiple_of(i * qc, 128), qc)],
                              q_all.at[pl.ds(pl.multiple_of(i * tok, 128), tok), :], local.at[2]),
        pltpu.make_async_copy(t_ref, t_all.at[i], local.at[3]),
        pltpu.make_async_copy(w_ref, wpair(z, i), local.at[4]),
    ]
    for cp in loc:
        cp.start()

    def w_src0(origin):
        return w_ref.at[pl.ds(pl.multiple_of(xh * half, 16), half), :]

    wz_ids = [(new_id(), new_id()) for _ in range(Z - 1)]
    kz_ids = [[(new_id(), new_id()) for _ in range(2)] for _ in range(Z - 1)]

    def wz(t):
        if t == 0:
            dst = lambda origin: wunit(origin, i, xh)
            return z_copies(wz_ids[0], w_src0, dst, 0)
        same = lambda origin: wunit(origin, i, xh)
        return z_copies(wz_ids[t], same, same, t)

    def kz(t, a):
        if online:
            ids = kz_ids[t][a]
            left_at = lambda n: kv_left[n].at[a] if n >= 0 else kv.at[a]
            right_at = lambda n: kv_right[n].at[a] if n >= 0 else kv.at[a]
            to_right = lambda: rcopy(ids[0], left_at(t - 1), left_at(t), g, s + cell)
            to_left = lambda: rcopy(ids[1], right_at(t - 1), right_at(t), g, s - cell)
            right = (has_right & (z - t >= 0), to_right)
            left = (has_left & (z + t <= Z - 1), to_left)
            return (right, left), ((z - 1 - t >= 0, to_right), (z + 1 + t <= Z - 1, to_left))
        return z_copies(kz_ids[t][a], lambda o: layer_rows(o, a), lambda o: layer_rows(o, a), t)

    for cond, make in wz(0)[0]:
        start_if(cond, make)

    kv_in = []
    for p in partners:
        for which, ref in ((0, k_ref), (1, v_ref)):
            n = new_id()

            def make(n=n, p=p, which=which, ref=ref):
                return rcopy(n, ref.at[:, :, pl.ds(pl.multiple_of(p * kc, 128), kc)],
                             own_blocks(which, i), g, z * cell + p)

            def landed(n=n, p=p, which=which):
                at = own_blocks(which, p)
                return rcopy(n, at, at, g, z * cell + p)

            start(make)
            kv_in.append(landed)
    def w_send(make_src, make_dst, gg, ss, make_land, cond=None):
        n = new_id()
        make = lambda: rcopy(n, make_src(), make_dst(), gg, ss)
        if cond is None:
            start(make)
        else:
            start_if(cond, make)
        return (cond, lambda: rcopy(n, make_land(), make_land(), gg, ss))

    yi = (1 - y) * 2 + c
    core_dev = z * cell + cores
    y_dev = z * cell + yi
    y_cores = (1 - y) * 2 + (1 - c)

    def send_core(origin, idx, xx, idx_there, xx_there, cond=None):
        return w_send(lambda: wunit(origin, idx, xx), lambda: wunit(origin, idx, xx), g, core_dev,
                      lambda: wunit(origin, idx_there, xx_there), cond)

    final, y_lands, q_in = [], [], []

    def send_own_weight():
        n_own = new_id()
        own_core = lambda: rcopy(n_own, w_ref, wpair(z, i), g, core_dev)
        start(own_core)
        final.append((None, lambda: rcopy(n_own, wpair(z, cores), wpair(z, cores), g, core_dev)))
        if Y == 2:
            y_lands.append((z, None, w_send(lambda: w_src0(z), lambda: wunit(z, i, xh), g, y_dev,
                                            lambda: wunit(z, yi, xh))))

    def send_queries():
        for p in partners:
            n = new_id()

            def make(n=n, p=p):
                return rcopy(n, q_ref.at[:, pl.ds(pl.multiple_of(p * qc, 128), qc)],
                             q_all.at[pl.ds(pl.multiple_of(i * tok, 128), tok), :], g, z * cell + p)

            def landed(n=n, p=p):
                at = q_all.at[pl.ds(pl.multiple_of(p * tok, 128), tok), :]
                return rcopy(n, at, at, g, z * cell + p)

            start(make)
            q_in.append(landed)
            m = new_id()

            def make_t(m=m, p=p):
                return rcopy(m, t_ref, t_all.at[i], g, z * cell + p)

            def landed_t(m=m, p=p):
                return rcopy(m, t_all.at[p], t_all.at[p], g, z * cell + p)

            start(make_t)
            q_in.append(landed_t)


    x_lands = []

    def spread(origin, cond):
        x_lands.append((origin, cond, i, w_send(
            lambda: wunit(origin, i, xh), lambda: wunit(origin, i, xh), gx, s,
            lambda: wunit(origin, i, 1 - xh), cond)))
        if Y == 2:
            y_lands.append((origin, cond, w_send(
                lambda: wunit(origin, i, xh), lambda: wunit(origin, i, xh), g, y_dev,
                lambda: wunit(origin, yi, xh), cond)))
        final.append(send_core(origin, i, xh, cores, xh, cond))

    def maybe_wait(entry):
        cond, make = entry
        if cond is None:
            make().wait_recv()
        else:
            wait_recv_if(cond, make)

    def relay_y(count=1 << 20):
        while y_lands and count > 0:
            count -= 1
            origin, cond, entry = y_lands.pop(0)
            maybe_wait(entry)
            x_lands.append((origin, cond, yi, w_send(
                lambda origin=origin: wunit(origin, yi, xh), lambda origin=origin: wunit(origin, yi, xh), gx, s,
                lambda origin=origin: wunit(origin, yi, 1 - xh), cond)))
            final.append(send_core(origin, yi, xh, y_cores, xh, cond))

    def relay_x(count=1 << 20):
        while x_lands and count > 0:
            count -= 1
            origin, cond, idx, entry = x_lands.pop(0)
            maybe_wait(entry)
            there = cores if idx is i else y_cores
            final.append(send_core(origin, idx, 1 - xh, there, 1 - xh, cond))

    def w_step(t):
        for cond, make in wz(t)[1]:
            wait_recv_if(cond, make)
        if t + 1 < Z - 1:
            for cond, make in wz(t + 1)[0]:
                start_if(cond, make)
        spread(z - 1 - t, z - 1 - t >= 0)
        spread(z + 1 + t, z + 1 + t <= Z - 1)

    def k_step(t):
        for a in (0, 1):
            for cond, make in kz(t, a)[1]:
                wait_recv_if(cond, make)
            if t + 1 < Z - 1:
                for cond, make in kz(t + 1, a)[0]:
                    start_if(cond, make)

    factor = HD ** -0.5 * LOG2E
    n_seq = Z * cell
    stride = n_seq // ENTRIES

    def softmax_pass(keys, vals, rows, hh, block, first, last):
        cols = [pl.ds((hh * gh + h) * HD, HD) for h in range(gh)]
        qq = jnp.concatenate([q_all[rows, cc] for cc in cols], 0)
        sc = lax.dot_general(keys, qq, (((1,), (1,)), ((), ())), preferred_element_type=jnp.float32)
        top = jnp.max(sc, axis=0, keepdims=True)
        if not first:
            before = m_ref[block]
            top = jnp.maximum(before, top)
        wts = jnp.exp2((sc - top) * factor)
        total = jnp.sum(wts, axis=0, keepdims=True)
        mixed = lax.dot_general(vals, wts.astype(jnp.bfloat16), (((0,), (0,)), ((), ())),
                                preferred_element_type=jnp.float32)
        if not first:
            shrink = jnp.exp2((before - top) * factor)
            total = total + l_ref[block] * shrink
            mixed = mixed + acc_ref[block] * shrink
        if last:
            mixed = mixed / total
            for h in range(gh):
                att[rows, cols[h]] = mixed[:, h * QB:(h + 1) * QB].T.astype(jnp.bfloat16)
        else:
            m_ref[block] = top
            l_ref[block] = total
            acc_ref[block] = mixed

    def attend(owner, parts, first, last):
        def step(b, carry):
            rows = pl.ds(pl.multiple_of(owner * tok + b * QB, QB), QB)
            if parts is None:
                picks = [(kv, t_smem[owner, b, e]) for e in range(ENTRIES)]
            else:
                base = z * cell + owner - lax.rem(b, 2) + n_seq
                picks = []
                for ref, layer in parts:
                    for r in range(cell // stride):
                        index = layer * cell + lax.rem(base, stride) + r * stride
                        e = lax.div(lax.rem(index - base + 2 * n_seq, n_seq), stride)
                        picks.append((ref, lax.rem(t_smem[owner, b, e], cell * nq)))
            for hh in range(hp):
                kcols = pl.ds(hh * HD, HD)
                keys = jnp.concatenate([ref[0, n, :, kcols] for ref, n in picks], 0)
                vals = jnp.concatenate([ref[1, n, :, kcols] for ref, n in picks], 0)
                softmax_pass(keys, vals, rows, hh, owner * nq + b, first, last)
            return carry

        lax.fori_loop(0, nq, step, 0)

    def attend_all(parts, first):
        def step(owner, carry):
            attend(owner, parts, first, False)
            return carry

        lax.fori_loop(0, cell, step, 0)

    def if_layer(layer):
        return pl.when(z == layer)

    def attend_last(owner):
        if not online:
            attend(owner, None, True, True)
            return
        for layer in range(Z):
            parts = brought(layer)[-1:]

            @if_layer(layer)
            def _(parts=parts):
                attend(owner, parts, False, True)

    def brought(layer):
        parts = []
        for t in range(Z - 1):
            if layer - 1 - t >= 0:
                parts.append((kv_left[t], layer - 1 - t))
            if layer + 1 + t < Z:
                parts.append((kv_right[t], layer + 1 + t))
        return parts

    def have_queries():
        for make in q_in:
            make().wait_recv()
        tcp = pltpu.make_async_copy(t_all, t_smem, local.at[5])
        tcp.start()
        tcp.wait()

    def start_keys():
        for cp in loc:
            cp.wait()
        for make in kv_in:
            make().wait_recv()
        for a in (0, 1):
            for cond, make in kz(0, a)[0]:
                start_if(cond, make)

    send_own_weight()
    w_step(0)
    if online:
        w_step(1)
        start_keys()
        relay_y(3)
        w_step(2)
        relay_y(2)
        k_step(0)
        relay_y()
        send_queries()
        relay_x(4)
        k_step(1)
        have_queries()
        for layer in range(Z):
            parts = [(kv, layer)] + brought(layer)[:-1]

            @if_layer(layer)
            def _(parts=parts):
                attend_all(parts, True)

        relay_x()
        k_step(2)
    else:
        start_keys()
        send_queries()
        for t in range(1, Z - 1):
            w_step(t)
        k_step(0)
        relay_y()
        for t in range(1, Z - 1):
            k_step(t)
        relay_x()
        have_queries()

    att_in = []
    for p in partners:
        attend_last(p)
        n = new_id()

        def make(n=n, p=p):
            return rcopy(n, att.at[pl.ds(pl.multiple_of(p * tok, 128), tok), :],
                         att_full.at[:, pl.ds(pl.multiple_of(i * qc, 128), qc)], g, z * cell + p)

        def landed(n=n, p=p):
            at = att_full.at[:, pl.ds(pl.multiple_of(p * qc, 128), qc)]
            return rcopy(n, at, at, g, z * cell + p)

        start(make)
        att_in.append(landed)
    relay_x()
    attend_last(i)
    own = pltpu.make_async_copy(att.at[pl.ds(pl.multiple_of(i * tok, 128), tok), :],
                                att_full.at[:, pl.ds(pl.multiple_of(i * qc, 128), qc)], local.at[6])
    own.start()
    own.wait()
    for make in att_in:
        make().wait_recv()
    for entry in final:
        maybe_wait(entry)

    for cond, make in pending:
        if cond is None:
            make().wait_send()
        else:
            @pl.when(cond)
            def _(make=make):
                make().wait_send()


def project(a_ref, w_ref, o_ref):
    o_ref[...] = jnp.dot(a_ref[...], w_ref[...], preferred_element_type=jnp.float32).astype(o_ref.dtype)


def body(Z, Y, queries, keys, values, block_table, out_weight):
    tok, width = queries.shape
    cell = 2 * Y
    hp = KVH // cell
    D = out_weight.shape[1]
    table = block_table
    online = Z == 4 and cell % (Z * cell // ENTRIES) == 0
    blocks_here = cell * tok // QB if online else 1
    rows = H // KVH * QB
    blocks = (tok // QB, QB, KVH * HD)
    part = (2, cell * tok // QB, QB, hp * HD)
    steps = Z - 1
    n_sems = steps * 6 + (cell - 1) * 5 + 8 + steps * 2 * 9
    flops = 4 * tok * H * ENTRIES * QB * HD
    depth = out_weight.shape[0] * Z * cell
    attended, weight = pl.pallas_call(
        functools.partial(kernel, Z, Y, online),
        out_shape=(
            jax.ShapeDtypeStruct((tok, width), jnp.bfloat16),
            jax.ShapeDtypeStruct((depth, D), jnp.bfloat16),
        ),
        in_specs=[pl.BlockSpec(memory_space=pl.ANY)] * 5,
        out_specs=(pl.BlockSpec(memory_space=pl.ANY), pl.BlockSpec(memory_space=pl.ANY)),
        scratch_shapes=[
            pltpu.VMEM((cell * tok, width // cell), jnp.bfloat16),
            pltpu.VMEM(part if online else (2, Z * cell * tok // QB, QB, hp * HD), jnp.bfloat16),
            [pltpu.VMEM(part, jnp.bfloat16)] * (steps if online else 0),
            [pltpu.VMEM(part, jnp.bfloat16)] * (steps if online else 0),
            pltpu.VMEM((cell,) + table.shape, jnp.int32),
            pltpu.SMEM((cell,) + table.shape, jnp.int32),
            pltpu.VMEM((cell * tok, width // cell), jnp.bfloat16),
            pltpu.VMEM((blocks_here, 1, rows), jnp.float32),
            pltpu.VMEM((blocks_here, 1, rows), jnp.float32),
            pltpu.VMEM((blocks_here, HD, rows), jnp.float32),
            pltpu.SemaphoreType.DMA((n_sems,)),
            pltpu.SemaphoreType.DMA((n_sems,)),
            pltpu.SemaphoreType.DMA((7,)),
        ],
        compiler_params=pltpu.CompilerParams(
            collective_id=0, has_side_effects=True, vmem_limit_bytes=58 * 1024 * 1024,
        ),
        cost_estimate=pl.CostEstimate(flops=flops, bytes_accessed=64 * 1024 * 1024, transcendentals=0),
    )(queries, keys.reshape(blocks), values.reshape(blocks), table, out_weight)
    tile = 512
    return pl.pallas_call(
        project,
        grid=(D // tile,),
        out_shape=jax.ShapeDtypeStruct((tok, D), jnp.bfloat16),
        in_specs=[
            pl.BlockSpec((tok, depth), lambda j: (0, 0)),
            pl.BlockSpec((depth, tile), lambda j: (0, j)),
        ],
        out_specs=pl.BlockSpec((tok, tile), lambda j: (0, j)),
        compiler_params=pltpu.CompilerParams(vmem_limit_bytes=60 * 1024 * 1024),
        cost_estimate=pl.CostEstimate(
            flops=2 * tok * depth * D, bytes_accessed=2 * (tok * depth + depth * D + tok * D), transcendentals=0),
    )(attended, weight)


def solution(mesh):
    groups, seq = mesh.shape["groups"], mesh.shape["seq"]
    Y = 2 if groups == 2 else 1
    Z = seq // (2 * Y)
    in_specs = (
        P(("groups", "seq"), None),
        P(("groups", "seq"), None),
        P(("groups", "seq"), None),
        P(("groups", "seq"), None),
        P("seq", None),
    )
    return jax.shard_map(
        functools.partial(body, Z, Y), mesh=mesh, in_specs=in_specs,
        out_specs=P(("groups", "seq"), None), check_vma=False,
    )
```

```python
import functools

import jax
import jax.numpy as jnp
from jax import lax
from jax.experimental import pallas as pl
from jax.experimental.pallas import tpu as pltpu
from jax.sharding import PartitionSpec as P

H = 16
KVH = 4
HD = 128
QB = 128
ENTRIES = 8
MESH = pl.DeviceIdType.MESH
LOG2E = 1.4426950408889634


def kernel(
    Z, Y, online, q_ref, k_ref, v_ref, t_ref, w_ref, att_full, w_all,
    q_all, kv, kv_left, kv_right, t_all, t_smem, att, m_ref, l_ref, acc_ref, send, recv, local,
):
    cell = 2 * Y
    hp = KVH // cell
    gh = H // KVH
    tok = q_ref.shape[0]
    nq = tok // QB
    wrows = w_ref.shape[0]
    half = wrows // 2
    qc = hp * gh * HD
    kc = hp * HD

    g = lax.axis_index("groups")
    s = lax.axis_index("seq")
    z = lax.div(s, cell)
    i = lax.rem(s, cell)
    y = lax.div(i, 2)
    c = lax.rem(i, 2)
    xh = lax.rem(g, 2)
    gx = g + 1 - 2 * xh

    def dev(dy, dc):
        yy = 1 - y if dy else y
        cc = 1 - c if dc else c
        return yy * 2 + cc

    cores = i - c + (1 - c)
    partners = [dev(dy, dc) for dy in range(Y - 1, -1, -1) for dc in (1, 0) if dy or dc]
    has_left = z > 0
    has_right = z < Z - 1

    counter = [0]

    def new_id():
        counter[0] += 1
        return counter[0] - 1

    def rcopy(n, src, dst, gg, ss):
        return pltpu.make_async_remote_copy(
            src_ref=src, dst_ref=dst, send_sem=send.at[n], recv_sem=recv.at[n],
            device_id=(gg, ss), device_id_type=MESH,
        )

    pending = []

    barrier = pltpu.get_barrier_semaphore()
    for p in partners:
        pl.semaphore_signal(barrier, inc=1, device_id=(g, z * cell + p), device_id_type=MESH)
    pl.semaphore_signal(barrier, inc=1, device_id=(gx, s), device_id_type=MESH)

    @pl.when(has_left)
    def _():
        pl.semaphore_signal(barrier, inc=1, device_id=(g, s - cell), device_id_type=MESH)

    @pl.when(has_right)
    def _():
        pl.semaphore_signal(barrier, inc=1, device_id=(g, s + cell), device_id_type=MESH)

    edges = jnp.where(has_left, 1, 0) + jnp.where(has_right, 1, 0)
    pl.semaphore_wait(barrier, len(partners) + 1 + edges)

    def wunit(origin, idx, xx, rows=None):
        start = (origin * cell + idx) * wrows + xx * half
        return w_all.at[pl.ds(pl.multiple_of(start, 16), half), :]

    def wpair(origin, idx):
        start = (origin * cell + idx) * wrows
        return w_all.at[pl.ds(pl.multiple_of(start, 16), wrows), :]

    def layer_rows(origin):
        n = cell * nq
        return kv.at[:, pl.ds(origin * n, n)]

    def own_blocks(which, idx):
        return kv.at[which, pl.ds((idx if online else z * cell + idx) * nq, nq)]

    def z_copies(ids, src_of, dst_of, t):
        right = (has_right & (z - t >= 0), lambda: rcopy(ids[0], src_of(z - t), dst_of(z - t), g, s + cell))
        left = (has_left & (z + t <= Z - 1), lambda: rcopy(ids[1], src_of(z + t), dst_of(z + t), g, s - cell))
        from_left = (z - 1 - t >= 0, lambda: rcopy(ids[0], dst_of(z - 1 - t), dst_of(z - 1 - t), g, s + cell))
        from_right = (z + 1 + t <= Z - 1, lambda: rcopy(ids[1], dst_of(z + 1 + t), dst_of(z + 1 + t), g, s - cell))
        return (right, left), (from_left, from_right)

    def start_if(cond, make):
        @pl.when(cond)
        def _():
            make().start()

        pending.append((cond, make))

    def start(make):
        make().start()
        pending.append((None, make))

    def wait_recv_if(cond, make):
        @pl.when(cond)
        def _():
            make().wait_recv()

    loc = [
        pltpu.make_async_copy(k_ref.at[:, :, pl.ds(pl.multiple_of(i * kc, 128), kc)],
                              own_blocks(0, i), local.at[0]),
        pltpu.make_async_copy(v_ref.at[:, :, pl.ds(pl.multiple_of(i * kc, 128), kc)],
                              own_blocks(1, i), local.at[1]),
        pltpu.make_async_copy(q_ref.at[:, pl.ds(pl.multiple_of(i * qc, 128), qc)],
                              q_all.at[pl.ds(pl.multiple_of(i * tok, 128), tok), :], local.at[2]),
        pltpu.make_async_copy(t_ref, t_all.at[i], local.at[3]),
        pltpu.make_async_copy(w_ref, wpair(z, i), local.at[4]),
    ]
    for cp in loc:
        cp.start()

    def w_src0(origin):
        return w_ref.at[pl.ds(pl.multiple_of(xh * half, 16), half), :]

    wz_ids = [(new_id(), new_id()) for _ in range(Z - 1)]
    kz_ids = [(new_id(), new_id()) for _ in range(Z - 1)]

    def wz(t):
        if t == 0:
            dst = lambda origin: wunit(origin, i, xh)
            return z_copies(wz_ids[0], w_src0, dst, 0)
        same = lambda origin: wunit(origin, i, xh)
        return z_copies(wz_ids[t], same, same, t)

    def kz(t):
        if online:
            ids = kz_ids[t]
            to_right = lambda: rcopy(ids[0], kv_left[t - 1] if t else kv, kv_left[t], g, s + cell)
            to_left = lambda: rcopy(ids[1], kv_right[t - 1] if t else kv, kv_right[t], g, s - cell)
            right = (has_right & (z - t >= 0), to_right)
            left = (has_left & (z + t <= Z - 1), to_left)
            return (right, left), ((z - 1 - t >= 0, to_right), (z + 1 + t <= Z - 1, to_left))
        return z_copies(kz_ids[t], layer_rows, layer_rows, t)

    for cond, make in wz(0)[0]:
        start_if(cond, make)

    kv_in = []
    for p in partners:
        for which, ref in ((0, k_ref), (1, v_ref)):
            n = new_id()

            def make(n=n, p=p, which=which, ref=ref):
                return rcopy(n, ref.at[:, :, pl.ds(pl.multiple_of(p * kc, 128), kc)],
                             own_blocks(which, i), g, z * cell + p)

            def landed(n=n, p=p, which=which):
                at = own_blocks(which, p)
                return rcopy(n, at, at, g, z * cell + p)

            start(make)
            kv_in.append(landed)
    def w_send(make_src, make_dst, gg, ss, make_land, cond=None):
        n = new_id()
        make = lambda: rcopy(n, make_src(), make_dst(), gg, ss)
        if cond is None:
            start(make)
        else:
            start_if(cond, make)
        return (cond, lambda: rcopy(n, make_land(), make_land(), gg, ss))

    yi = (1 - y) * 2 + c
    core_dev = z * cell + cores
    y_dev = z * cell + yi
    y_cores = (1 - y) * 2 + (1 - c)

    def send_core(origin, idx, xx, idx_there, xx_there, cond=None):
        return w_send(lambda: wunit(origin, idx, xx), lambda: wunit(origin, idx, xx), g, core_dev,
                      lambda: wunit(origin, idx_there, xx_there), cond)

    final, y_lands, q_in = [], [], []

    def send_rest():
        n_own = new_id()
        own_core = lambda: rcopy(n_own, w_ref, wpair(z, i), g, core_dev)
        start(own_core)
        final.append((None, lambda: rcopy(n_own, wpair(z, cores), wpair(z, cores), g, core_dev)))
        if Y == 2:
            y_lands.append((z, None, w_send(lambda: w_src0(z), lambda: wunit(z, i, xh), g, y_dev,
                                            lambda: wunit(z, yi, xh))))
        for p in partners:
            n = new_id()

            def make(n=n, p=p):
                return rcopy(n, q_ref.at[:, pl.ds(pl.multiple_of(p * qc, 128), qc)],
                             q_all.at[pl.ds(pl.multiple_of(i * tok, 128), tok), :], g, z * cell + p)

            def landed(n=n, p=p):
                at = q_all.at[pl.ds(pl.multiple_of(p * tok, 128), tok), :]
                return rcopy(n, at, at, g, z * cell + p)

            start(make)
            q_in.append(landed)
            m = new_id()

            def make_t(m=m, p=p):
                return rcopy(m, t_ref, t_all.at[i], g, z * cell + p)

            def landed_t(m=m, p=p):
                return rcopy(m, t_all.at[p], t_all.at[p], g, z * cell + p)

            start(make_t)
            q_in.append(landed_t)


    x_lands = []

    def spread(origin, cond):
        x_lands.append((origin, cond, i, w_send(
            lambda: wunit(origin, i, xh), lambda: wunit(origin, i, xh), gx, s,
            lambda: wunit(origin, i, 1 - xh), cond)))
        if Y == 2:
            y_lands.append((origin, cond, w_send(
                lambda: wunit(origin, i, xh), lambda: wunit(origin, i, xh), g, y_dev,
                lambda: wunit(origin, yi, xh), cond)))
        final.append(send_core(origin, i, xh, cores, xh, cond))

    def maybe_wait(entry):
        cond, make = entry
        if cond is None:
            make().wait_recv()
        else:
            wait_recv_if(cond, make)

    def relay_y(count=1 << 20):
        while y_lands and count > 0:
            count -= 1
            origin, cond, entry = y_lands.pop(0)
            maybe_wait(entry)
            x_lands.append((origin, cond, yi, w_send(
                lambda origin=origin: wunit(origin, yi, xh), lambda origin=origin: wunit(origin, yi, xh), gx, s,
                lambda origin=origin: wunit(origin, yi, 1 - xh), cond)))
            final.append(send_core(origin, yi, xh, y_cores, xh, cond))

    def relay_x(count=1 << 20):
        while x_lands and count > 0:
            count -= 1
            origin, cond, idx, entry = x_lands.pop(0)
            maybe_wait(entry)
            there = cores if idx is i else y_cores
            final.append(send_core(origin, idx, 1 - xh, there, 1 - xh, cond))

    def w_step(t):
        for cond, make in wz(t)[1]:
            wait_recv_if(cond, make)
        if t + 1 < Z - 1:
            for cond, make in wz(t + 1)[0]:
                start_if(cond, make)
        spread(z - 1 - t, z - 1 - t >= 0)
        spread(z + 1 + t, z + 1 + t <= Z - 1)

    def k_step(t):
        for cond, make in kz(t)[1]:
            wait_recv_if(cond, make)
        if t + 1 < Z - 1:
            for cond, make in kz(t + 1)[0]:
                start_if(cond, make)

    factor = HD ** -0.5 * LOG2E
    n_seq = Z * cell
    stride = n_seq // ENTRIES

    def softmax_pass(keys, vals, rows, hh, block, first, last):
        cols = [pl.ds((hh * gh + h) * HD, HD) for h in range(gh)]
        qq = jnp.concatenate([q_all[rows, cc] for cc in cols], 0)
        sc = lax.dot_general(keys, qq, (((1,), (1,)), ((), ())), preferred_element_type=jnp.float32)
        top = jnp.max(sc, axis=0, keepdims=True)
        if not first:
            before = m_ref[block]
            top = jnp.maximum(before, top)
        wts = jnp.exp2((sc - top) * factor)
        total = jnp.sum(wts, axis=0, keepdims=True)
        mixed = lax.dot_general(vals, wts.astype(jnp.bfloat16), (((0,), (0,)), ((), ())),
                                preferred_element_type=jnp.float32)
        if not first:
            shrink = jnp.exp2((before - top) * factor)
            total = total + l_ref[block] * shrink
            mixed = mixed + acc_ref[block] * shrink
        if last:
            mixed = mixed / total
            for h in range(gh):
                att[rows, cols[h]] = mixed[:, h * QB:(h + 1) * QB].T.astype(jnp.bfloat16)
        else:
            m_ref[block] = top
            l_ref[block] = total
            acc_ref[block] = mixed

    def attend(owner, parts, first, last):
        def step(b, carry):
            rows = pl.ds(pl.multiple_of(owner * tok + b * QB, QB), QB)
            if parts is None:
                picks = [(kv, t_smem[owner, b, e]) for e in range(ENTRIES)]
            else:
                base = z * cell + owner - lax.rem(b, 2) + n_seq
                picks = []
                for ref, layer in parts:
                    for r in range(cell // stride):
                        index = layer * cell + lax.rem(base, stride) + r * stride
                        e = lax.div(lax.rem(index - base + 2 * n_seq, n_seq), stride)
                        picks.append((ref, lax.rem(t_smem[owner, b, e], cell * nq)))
            for hh in range(hp):
                kcols = pl.ds(hh * HD, HD)
                keys = jnp.concatenate([ref[0, n, :, kcols] for ref, n in picks], 0)
                vals = jnp.concatenate([ref[1, n, :, kcols] for ref, n in picks], 0)
                softmax_pass(keys, vals, rows, hh, owner * nq + b, first, last)
            return carry

        lax.fori_loop(0, nq, step, 0)

    def attend_all(parts, first):
        def step(owner, carry):
            attend(owner, parts, first, False)
            return carry

        lax.fori_loop(0, cell, step, 0)

    def if_layer(layer):
        return pl.when(z == layer)

    def attend_last(owner):
        if not online:
            attend(owner, None, True, True)
            return
        for layer in range(Z):
            near = first_parts(layer)
            parts = [part for part in brought(layer) if part[1] not in [p[1] for p in near]]
            if layer in (0, Z - 1):
                parts = parts[-1:]

            @if_layer(layer)
            def _(parts=parts):
                attend(owner, parts, False, True)

    def brought(layer):
        parts = []
        for t in range(Z - 1):
            if layer - 1 - t >= 0:
                parts.append((kv_left[t], layer - 1 - t))
            if layer + 1 + t < Z:
                parts.append((kv_right[t], layer + 1 + t))
        return parts

    def first_parts(layer):
        return [(kv, layer), brought(layer)[0]]

    def have_queries():
        for make in q_in:
            make().wait_recv()
        tcp = pltpu.make_async_copy(t_all, t_smem, local.at[5])
        tcp.start()
        tcp.wait()

    for cp in loc[:2]:
        cp.wait()
    for make in kv_in:
        make().wait_recv()
    for cond, make in kz(0)[0]:
        start_if(cond, make)
    send_rest()
    w_step(0)
    for cp in loc[2:]:
        cp.wait()
    if online:
        w_step(1)
        relay_y(1)
        w_step(2)
        k_step(0)
        relay_y(2)
        have_queries()
        for layer in range(Z):
            parts = first_parts(layer)

            @if_layer(layer)
            def _(parts=parts):
                attend_all(parts, True)

        k_step(1)
        relay_y()
        relay_x(5)
        for layer, part in ((0, (kv_right[1], 2)), (Z - 1, (kv_left[1], Z - 3))):

            @if_layer(layer)
            def _(part=part):
                attend_all([part], False)

        relay_x(4)
        k_step(2)
    else:
        for t in range(1, Z - 1):
            w_step(t)
        k_step(0)
        relay_y()
        for t in range(1, Z - 1):
            k_step(t)
        relay_x()
        have_queries()

    att_in = []
    for p in partners:
        attend_last(p)
        n = new_id()

        def make(n=n, p=p):
            return rcopy(n, att.at[pl.ds(pl.multiple_of(p * tok, 128), tok), :],
                         att_full.at[:, pl.ds(pl.multiple_of(i * qc, 128), qc)], g, z * cell + p)

        def landed(n=n, p=p):
            at = att_full.at[:, pl.ds(pl.multiple_of(p * qc, 128), qc)]
            return rcopy(n, at, at, g, z * cell + p)

        start(make)
        att_in.append(landed)
    relay_x()
    attend_last(i)
    own = pltpu.make_async_copy(att.at[pl.ds(pl.multiple_of(i * tok, 128), tok), :],
                                att_full.at[:, pl.ds(pl.multiple_of(i * qc, 128), qc)], local.at[6])
    own.start()
    own.wait()
    for make in att_in:
        make().wait_recv()
    for entry in final:
        maybe_wait(entry)

    for cond, make in pending:
        if cond is None:
            make().wait_send()
        else:
            @pl.when(cond)
            def _(make=make):
                make().wait_send()


def project(a_ref, w_ref, o_ref):
    o_ref[...] = jnp.dot(a_ref[...], w_ref[...], preferred_element_type=jnp.float32).astype(o_ref.dtype)


def body(Z, Y, queries, keys, values, block_table, out_weight):
    tok, width = queries.shape
    cell = 2 * Y
    hp = KVH // cell
    D = out_weight.shape[1]
    table = block_table
    online = Z == 4 and cell % (Z * cell // ENTRIES) == 0
    blocks_here = cell * tok // QB if online else 1
    rows = H // KVH * QB
    blocks = (tok // QB, QB, KVH * HD)
    part = (2, cell * tok // QB, QB, hp * HD)
    steps = Z - 1
    n_sems = steps * 4 + (cell - 1) * 5 + 8 + steps * 2 * 9
    flops = 4 * tok * H * ENTRIES * QB * HD
    depth = out_weight.shape[0] * Z * cell
    attended, weight = pl.pallas_call(
        functools.partial(kernel, Z, Y, online),
        out_shape=(
            jax.ShapeDtypeStruct((tok, width), jnp.bfloat16),
            jax.ShapeDtypeStruct((depth, D), jnp.bfloat16),
        ),
        in_specs=[pl.BlockSpec(memory_space=pl.ANY)] * 5,
        out_specs=(pl.BlockSpec(memory_space=pl.ANY), pl.BlockSpec(memory_space=pl.ANY)),
        scratch_shapes=[
            pltpu.VMEM((cell * tok, width // cell), jnp.bfloat16),
            pltpu.VMEM(part if online else (2, Z * cell * tok // QB, QB, hp * HD), jnp.bfloat16),
            [pltpu.VMEM(part, jnp.bfloat16)] * (steps if online else 0),
            [pltpu.VMEM(part, jnp.bfloat16)] * (steps if online else 0),
            pltpu.VMEM((cell,) + table.shape, jnp.int32),
            pltpu.SMEM((cell,) + table.shape, jnp.int32),
            pltpu.VMEM((cell * tok, width // cell), jnp.bfloat16),
            pltpu.VMEM((blocks_here, 1, rows), jnp.float32),
            pltpu.VMEM((blocks_here, 1, rows), jnp.float32),
            pltpu.VMEM((blocks_here, HD, rows), jnp.float32),
            pltpu.SemaphoreType.DMA((n_sems,)),
            pltpu.SemaphoreType.DMA((n_sems,)),
            pltpu.SemaphoreType.DMA((7,)),
        ],
        compiler_params=pltpu.CompilerParams(
            collective_id=0, has_side_effects=True, vmem_limit_bytes=58 * 1024 * 1024,
        ),
        cost_estimate=pl.CostEstimate(flops=flops, bytes_accessed=64 * 1024 * 1024, transcendentals=0),
    )(queries, keys.reshape(blocks), values.reshape(blocks), table, out_weight)
    tile = 1024
    return pl.pallas_call(
        project,
        grid=(D // tile,),
        out_shape=jax.ShapeDtypeStruct((tok, D), jnp.bfloat16),
        in_specs=[
            pl.BlockSpec((tok, depth), lambda j: (0, 0)),
            pl.BlockSpec((depth, tile), lambda j: (0, j)),
        ],
        out_specs=pl.BlockSpec((tok, tile), lambda j: (0, j)),
        compiler_params=pltpu.CompilerParams(vmem_limit_bytes=60 * 1024 * 1024),
        cost_estimate=pl.CostEstimate(
            flops=2 * tok * depth * D, bytes_accessed=2 * (tok * depth + depth * D + tok * D), transcendentals=0),
    )(attended, weight)


def solution(mesh):
    groups, seq = mesh.shape["groups"], mesh.shape["seq"]
    Y = 2 if groups == 2 else 1
    Z = seq // (2 * Y)
    in_specs = (
        P(("groups", "seq"), None),
        P(("groups", "seq"), None),
        P(("groups", "seq"), None),
        P(("groups", "seq"), None),
        P("seq", None),
    )
    return jax.shard_map(
        functools.partial(body, Z, Y), mesh=mesh, in_specs=in_specs,
        out_specs=P(("groups", "seq"), None), check_vma=False,
    )
```
